512 devices in a mesh: dp: 64 (over z, x_hi, core), param: 8 (over x_lo, y).
Axes of the slice: x: 4 (x_hi: 2, x_lo: 2; x = x_hi * 2 + x_lo), y: 4, z: 16, core: 2. Of those that a mesh axis runs over, the one named last changes fastest.
Arguments:
- output_gradient: bfloat16 [65536, 4096], P('dp', 'param'), may hold values from -6 to 6
- adapter_activations: bfloat16 [65536, 64], P('dp'), may hold values from -6 to 6
- proj: bfloat16 [4096, 64, 4096], P(('param', 'dp')), may hold values from -0.01171875 to 0.01171875
- labels: int32 [256], P('dp'), may hold values from 0 to 31
Outputs:
- scores: float32 [256, 32], P('dp')
- task_means: float32 [32, 4096], P(None, 'param')
The draws below stay inside these ranges and needn't reach their ends.
All inputs are finite; a program needn't handle non-finite values.
Results may differ from the reference program's by a relative error of at most 0.0029.
Values may be sent and summed in bfloat16 or wider, within the bound.
A program may use at most 64 MiB of HBM per device.

```python
import math
import jax
import jax.numpy as jnp
import numpy as np
from jax import lax

DO = 4096
ADAPTER_RANK = 64
K = 4096
NT = 32
EXAMPLE_LENGTH = 256
EXAMPLE_COUNT = 256
POOL_TOKENS = 65536


def with_ends(array, own_key, smallest, high):
    spot = [jax.random.randint(jax.random.fold_in(own_key, axis), (), 0, length) for axis, length in enumerate(array.shape)]
    widest = array.shape.index(max(array.shape))
    beside = spot[:widest] + [(spot[widest] + 1) % array.shape[widest]] + spot[widest + 1:]
    return array.at[tuple(spot)].set(smallest).at[tuple(beside)].set(high)


def block_levels(own_key, shape, split, low, top_value):
    loudness, own = 1.0, jax.random.fold_in(own_key, 6)
    for axis_at, parts in split:
        heights = jnp.exp(jax.random.uniform(jax.random.fold_in(own, axis_at), (parts,), jnp.float32, low / len(split), top_value / len(split)))
        loudness = loudness * jnp.repeat(heights, shape[axis_at] // parts).reshape([-1 if axis == axis_at else 1 for axis in range(len(shape))])
    return loudness


def cumulative_ranks(number_of, slope):
    portions = [(1 << 20) // math.isqrt(rank ** slope) + 1 for rank in range(1, number_of + 1)]
    spread = 1 + sum(portions) // (1 << 30)
    return np.cumsum(np.array([max(1, weight // spread) for weight in portions]))


def ranked_ids(own_key, dims, count, slope):
    table = cumulative_ranks(count, slope)
    lot = jax.random.randint(jax.random.fold_in(own_key, 1), dims, 0, int(table[count - 1]))
    rank = jnp.searchsorted(jnp.asarray(table, jnp.int32), lot, side="right")
    return jax.random.permutation(jax.random.fold_in(own_key, 2), count)[rank].astype(jnp.int32)


def gaussian(rng, dims, scale, bound, shards=(), kind=jnp.bfloat16):
    array = jax.random.normal(rng, dims, jnp.float32) * scale
    if len(shards) > 0:
        array = block_levels(rng, dims, shards, -0.22, 0.18) * array
    return jnp.clip(array, min=-bound, max=bound).astype(kind)


def setup_inputs(seed: int = 0) -> dict:
    splits = jax.random.split(jax.random.key(seed), 5)
    output_gradient = gaussian(splits[0], (POOL_TOKENS, DO), 1.0, 6.0, ((0, 64), (1, 8)))
    adapter_activations = gaussian(splits[1], (POOL_TOKENS, ADAPTER_RANK), 1.0, 6.0, ((0, 64),))
    proj = gaussian(splits[2], (DO, ADAPTER_RANK, K), (DO * ADAPTER_RANK) ** -0.5, 0.01171875, ((0, 512),))
    labels = with_ends(ranked_ids(splits[3], (EXAMPLE_COUNT,), NT, 2), jax.random.fold_in(splits[3], 3), 0, NT - 1).astype(jnp.int32)
    return {"output_gradient": output_gradient, "adapter_activations": adapter_activations, "proj": proj, "labels": labels}


epsilon = 1e-06

def reference(output_gradient, adapter_activations, proj, labels):
    grad_tok = output_gradient.astype(jnp.float32).reshape(EXAMPLE_COUNT, EXAMPLE_LENGTH, DO)
    activation_tokens = adapter_activations.astype(jnp.float32).reshape(EXAMPLE_COUNT, EXAMPLE_LENGTH, ADAPTER_RANK)
    gradient = jnp.einsum('eto,etr->eor', grad_tok, activation_tokens).astype(jnp.bfloat16)
    projected = jnp.dot(gradient.reshape(EXAMPLE_COUNT, DO * ADAPTER_RANK), proj.reshape(DO * ADAPTER_RANK, K), preferred_element_type=jnp.float32)
    onehot = (labels[:, None] == jnp.arange(NT, dtype=jnp.int32)[None, :]).astype(jnp.float32)
    totals = jnp.dot(onehot.T, projected, precision=lax.Precision.HIGHEST)
    counts = lax.optimization_barrier(jnp.sum(onehot, axis=0))
    task_means = totals / jnp.maximum(counts, 1.0)[:, None]
    score_dots = jnp.dot(projected, task_means.T, precision=lax.Precision.HIGHEST)
    grad_sq = lax.optimization_barrier(jnp.sum(projected * projected, axis=1))
    mean_sq = lax.optimization_barrier(jnp.sum(task_means * task_means, axis=1))
    scores = score_dots / K * lax.rsqrt(grad_sq / K + epsilon)[:, None] * lax.rsqrt(mean_sq / K + epsilon)[None, :]
    return (scores, task_means)
```

```python
import functools

import jax
import jax.numpy as jnp
from jax import lax
from jax.experimental import pallas as pl
from jax.experimental.pallas import tpu as pltpu
from jax.sharding import PartitionSpec as P

K = 4096
NT = 32
EPSILON = 1e-06
MESH = pl.DeviceIdType.MESH
F32 = jnp.float32
BF16 = jnp.bfloat16
HIGHEST = lax.Precision.HIGHEST

OFFSETS = (0, 8, 1, 15, 7, 9, 2, 14, 6, 10, 3, 13, 5, 11, 4, 12)
GROUPS = 4


def kernel(
    og_h, act_h, proj_h, lab_ref, scores_ref, means_ref,
    og_v, act_v, proj_v, g32, s32, qs, rq, rb, f32s, ls, lr,
    own, cs, cr, ao, bo, sa, ra, sb, rbb, sa2, ra2, sb2, rb2,
    dsum, zs32, zs, zr, tsum, zts, ztr, qas, qar, agr, pks, pkr,
    in_sem, loc_sem, lab_sem, quad_sem, zg_send, zg_recv, core_sem,
    xa_sem, yb_sem, ya_sem, xb_sem, zs_send, zs_recv, zt_sem, qa_sem, ag_sem, pk_sem,
):
    nz = 16
    per = nz // GROUPS
    rw = per * 4
    dp, param = lax.axis_index("dp"), lax.axis_index("param")
    z, q = dp // 4, dp % 4
    xl, y = param // 4, param % 4

    def xor(value, bits):
        out = value
        if bits & 1:
            out = out + 1 - 2 * (value % 2)
        if bits & 2:
            out = out + 2 - 4 * ((value // 2) % 2)
        if bits & 4:
            out = out + 4 - 8 * ((value // 4) % 2)
        return out

    def ahead(i):
        return ((z + OFFSETS[i]) % nz) * 4 + q

    def behind(i):
        return ((z + nz - OFFSETS[i]) % nz) * 4 + q

    def x_peer(a):
        return (xor(dp, a & 2), xor(param, (a & 1) * 4))

    def y_peer(r):
        return (dp, xor(param, r))

    def remote(src, dst, send, recv, device):
        return pltpu.make_async_remote_copy(
            src_ref=src, dst_ref=dst, send_sem=send, recv_sem=recv,
            device_id=device, device_id_type=MESH,
        )

    def wait_all(ref, sem):
        pltpu.make_async_copy(ref, ref, sem).wait()

    barrier = pltpu.get_barrier_semaphore()
    peers = [(xor(dp, s), param) for s in (1, 2, 3)]
    peers += [(ahead(i), param) for i in range(1, nz)]
    peers += [(dp, xor(param, r)) for r in range(1, 8)]
    peers += [x_peer(3)]
    for peer in peers:
        pl.semaphore_signal(barrier, inc=1, device_id=peer, device_id_type=MESH)

    act_in = pltpu.make_async_copy(act_h, act_v, in_sem.at[0])
    act_in.start()
    og_in = []
    for m in range(4):
        copy = pltpu.make_async_copy(
            og_h.at[pl.ds(m * 256, 256)], og_v.at[pl.ds(m * 256, 256)], in_sem.at[2 + m]
        )
        copy.start()
        og_in.append(copy)
    proj_in = pltpu.make_async_copy(proj_h, proj_v, in_sem.at[1])
    proj_in.start()

    lane = lax.broadcasted_iota(jnp.int32, (1, 128), 1)
    label_row = jnp.zeros((1, 128), jnp.int32)
    for m in range(4):
        label_row = jnp.where(lane % 4 == m, lab_ref[0:1, m : m + 1], label_row)
    ls[...] = label_row

    act_in.wait()
    low = lax.broadcasted_iota(jnp.int32, (64, 128), 1) < 64
    for m in range(4):
        og_in[m].wait()
        act = act_v[m * 256 : (m + 1) * 256, :]
        g32[m] = lax.dot_general(
            og_v[m * 256 : (m + 1) * 256, :],
            jnp.concatenate([act, act], axis=1),
            (((0,), (0,)), ((), ())),
            preferred_element_type=F32,
        )
        for j in range(4):
            even = g32[m, pl.ds(2 * j, 64, stride=8), :]
            odd = g32[m, pl.ds(2 * j + 1, 64, stride=8), :]
            s32[pl.ds(m * 4 + j, 64, stride=16), :] = jnp.where(low, even, odd)
    for block in range(nz):
        qs[block] = s32[block * 64 : (block + 1) * 64, :].astype(BF16).reshape(4, 16, 128)

    pl.semaphore_wait(barrier, len(peers))

    quad = []
    for s in (1, 2, 3):
        copy = remote(
            qs.at[:, xor(q, s)], rq.at[:, s], quad_sem.at[0, s], quad_sem.at[1, s], (xor(dp, s), param)
        )
        copy.start()
        quad.append(copy)
    mine = pltpu.make_async_copy(qs.at[:, q], rq.at[:, 0], loc_sem.at[0])
    mine.start()
    labels = []
    for i in range(1, nz):
        copy = remote(ls, lr.at[i], lab_sem.at[0], lab_sem.at[1], (ahead(i), param))
        copy.start()
    lr[0] = label_row
    mine.wait()
    for copy in quad:
        copy.wait()

    home = pltpu.make_async_copy(rq.at[z], rb.at[0], loc_sem.at[1])
    home.start()
    for i in range(1, nz):
        remote(
            rq.at[ahead(i) // 4], rb.at[i], zg_send, zg_recv.at[i // per], (ahead(i), param)
        ).start()
    home.wait()
    proj_in.wait()

    def project(c):
        first = max(1, c * per)
        wait_all(rb.at[pl.ds(first, (c + 1) * per - first)], zg_recv.at[c])
        for s in range(4):
            for k in range(per):
                at = (s * per + k) * 16
                f32s[c, at : at + 16, :] = rb[c * per + k, s].astype(F32)
        rows = jnp.concatenate(
            [f32s[c, pl.ds(j, 4 * rw, stride=4), :].astype(BF16) for j in range(4)], axis=1
        )
        for x in range(2):
            for r in range(4):
                column = xor(xl, x) * 4 + xor(y, r)
                part = jnp.dot(
                    rows,
                    proj_v[:, pl.ds(pl.multiple_of(column * 512, 512), 512)],
                    preferred_element_type=F32,
                )
                for h in range(2):
                    own[c, h * 2 + x, r] = part[2 * h * rw : (2 * h + 1) * rw]
                    cs[c, h * 2 + x, r] = part[(2 * h + 1) * rw : (2 * h + 2) * rw].astype(BF16)
        remote(
            cs.at[c], cr.at[c], core_sem.at[0, c], core_sem.at[1, c], (xor(dp, 1), param)
        ).start()

    def after_core(c):
        wait_all(cr.at[c], core_sem.at[1, c])
        for a in range(4):
            for r in range(4):
                total = own[c, a, r] + cr[c, a, r].astype(F32)
                if a == 0:
                    ao[c, r] = total[:, :256]
                else:
                    sa[c, a - 1, r] = total[:, :256].astype(BF16)
                if r == 0:
                    bo[c, a] = total[:, 256:]
                else:
                    sb[c, r - 1, a] = total[:, 256:].astype(BF16)
        for n in (1, 2, 3):
            remote(sa.at[c, n - 1], ra.at[c, n - 1], xa_sem.at[0, c], xa_sem.at[1, c], x_peer(n)).start()
            remote(sb.at[c, n - 1], rbb.at[c, n - 1], yb_sem.at[0, c], yb_sem.at[1, c], y_peer(n)).start()

    def after_first(c):
        wait_all(ra.at[c], xa_sem.at[1, c])
        for r in (1, 2, 3, 0):
            total = ao[c, r]
            for n in range(3):
                total += ra[c, n, r].astype(F32)
            if r == 0:
                ao[c, 0] = total
            else:
                sa2[c, r - 1] = total
        for n in (1, 2, 3):
            remote(sa2.at[c, n - 1], ra2.at[c, n - 1], ya_sem.at[0, c], ya_sem.at[1, c], y_peer(n)).start()
        wait_all(rbb.at[c], yb_sem.at[1, c])
        for a in (1, 2, 3, 0):
            total = bo[c, a]
            for n in range(3):
                total += rbb[c, n, a].astype(F32)
            if a == 0:
                bo[c, 0] = total
            else:
                sb2[c, a - 1] = total
        for n in (1, 2, 3):
            remote(sb2.at[c, n - 1], rb2.at[c, n - 1], xb_sem.at[0, c], xb_sem.at[1, c], x_peer(n)).start()

    def after_second(c):
        wait_all(ra2.at[c], ya_sem.at[1, c])
        total = ao[c, 0] + ra2[c, 0] + ra2[c, 1] + ra2[c, 2]
        dsum[0, c * rw : (c + 1) * rw, :] = total[:, :128]
        dsum[1, c * rw : (c + 1) * rw, :] = total[:, 128:]
        wait_all(rb2.at[c], xb_sem.at[1, c])
        total = bo[c, 0] + rb2[c, 0] + rb2[c, 1] + rb2[c, 2]
        dsum[2, c * rw : (c + 1) * rw, :] = total[:, :128]
        dsum[3, c * rw : (c + 1) * rw, :] = total[:, 128:]

    def send_examples(c):
        base = c * per * 16
        for j in range(4):
            for m in range(4):
                zs32[pl.ds(base + j * 4 + m, per, stride=16), :] = dsum[
                    j, pl.ds(c * rw + m, per, stride=4), :
                ]
        for k in range(per):
            i = c * per + k
            zs[i] = zs32[i * 16 : (i + 1) * 16, :].astype(BF16)
        for i in range(max(1, c * per), (c + 1) * per):
            remote(zs.at[i], zr.at[i], zs_send, zs_recv, (behind(i), param)).start()

    for step in range(GROUPS + 2):
        if 0 <= step - 3 < GROUPS:
            after_second(step - 3)
            send_examples(step - 3)
        if 0 <= step - 2 < GROUPS:
            after_first(step - 2)
        if 0 <= step - 1 < GROUPS:
            after_core(step - 1)
        if step < GROUPS:
            project(step)
    after_second(GROUPS - 1)

    wait_all(lr.at[pl.ds(1, nz - 1)], lab_sem.at[1])
    all_labels = jnp.zeros((1, 128), jnp.int32)
    for i in range(nz):
        all_labels = jnp.where(lane // 4 == i, lr[i], all_labels)
    all_labels = jnp.where(lane < 4 * nz, all_labels, -1)
    row = lax.broadcasted_iota(jnp.int32, (NT, 4 * nz), 0)
    tag = row % 2
    for i in range(nz):
        tag = jnp.where(row // 2 == i, row % 2 + 2 * (behind(i) // 4), tag)
    onehot = (tag == all_labels[:, : 4 * nz]).astype(F32)
    for j in range(4):
        tsum[j] = jnp.dot(onehot, dsum[j], precision=HIGHEST, preferred_element_type=F32)
        for t in range(2):
            zts[pl.ds(2 * j + t, nz, stride=8), :] = tsum[j, pl.ds(t, nz, stride=2), :]
    for i in range(1, nz):
        remote(zts.at[pl.ds(i * 8, 8)], ztr.at[i], zt_sem.at[0], zt_sem.at[1], (behind(i), param)).start()
    send_examples(GROUPS - 1)

    pair = lax.broadcasted_iota(jnp.int32, (8, 128), 0) % 2 + 2 * z
    counts = jnp.sum((pair == all_labels).astype(F32), axis=1, keepdims=True)
    wait_all(ztr.at[pl.ds(1, nz - 1)], zt_sem.at[1])
    pair_total = zts[0:8, :]
    for i in range(1, nz):
        pair_total += ztr[i]
    qas[0] = pair_total
    qas[1] = jnp.broadcast_to(counts, (8, 128))
    for s in (1, 2, 3):
        remote(qas, qar.at[s - 1], qa_sem.at[0], qa_sem.at[1], (xor(dp, s), param)).start()
    wait_all(qar, qa_sem.at[1])
    pair_total = qas[0] + qar[0, 0] + qar[1, 0] + qar[2, 0]
    pair_count = qas[1] + qar[0, 1] + qar[1, 1] + qar[2, 1]
    mine8 = pl.multiple_of(z * 8, 8)
    agr[pl.ds(mine8, 8), :] = pair_total / jnp.maximum(pair_count, 1.0)
    for i in range(1, nz):
        remote(
            agr.at[pl.ds(mine8, 8)], agr.at[pl.ds(mine8, 8)], ag_sem.at[0], ag_sem.at[1], (ahead(i), param)
        ).start()

    wait_all(zr.at[pl.ds(1, nz - 1)], zs_recv)
    mine16 = zs32[0:16, :]
    for i in range(1, nz):
        mine16 += zr[i].astype(F32)

    wait_all(agr.at[pl.ds(0, (nz - 1) * 8)], ag_sem.at[1])
    dots = jnp.zeros((4, NT), F32)
    mean_sq = jnp.zeros((4, NT), F32)
    grad_sq = jnp.zeros((4, 128), F32)
    ones = jnp.ones((4, 128), F32)
    contract = (((1,), (1,)), ((), ()))
    for j in range(4):
        for t in range(2):
            tsum[j, pl.ds(t, nz, stride=2), :] = agr[pl.ds(2 * j + t, nz, stride=8), :]
        means = tsum[j]
        means_ref[:, j * 128 : (j + 1) * 128] = means
        part = mine16[j * 4 : (j + 1) * 4, :]
        dots += lax.dot_general(part, means, contract, precision=HIGHEST, preferred_element_type=F32)
        mean_sq += lax.dot_general(ones, means * means, contract, precision=HIGHEST, preferred_element_type=F32)
        grad_sq += part * part
    grad_sq = jnp.sum(grad_sq, axis=1, keepdims=True)
    pks[...] = jnp.zeros((8, 128), F32)
    pks[0:4, 0:NT] = dots
    pks[4:8, 0:NT] = mean_sq
    pks[0:4, 64:128] = jnp.broadcast_to(grad_sq, (4, 64))
    for n in range(1, 8):
        remote(pks, pkr.at[n - 1], pk_sem.at[0], pk_sem.at[1], (dp, xor(param, n))).start()
    wait_all(rb.at[pl.ds(1, nz - 1)], zg_send)
    wait_all(lr.at[pl.ds(1, nz - 1)], lab_sem.at[0])
    for c in range(GROUPS):
        wait_all(cs.at[c], core_sem.at[0, c])
        wait_all(sa.at[c], xa_sem.at[0, c])
        wait_all(sb.at[c], yb_sem.at[0, c])
        wait_all(sa2.at[c], ya_sem.at[0, c])
        wait_all(sb2.at[c], xb_sem.at[0, c])
    wait_all(zs.at[pl.ds(1, nz - 1)], zs_send)
    wait_all(ztr.at[pl.ds(1, nz - 1)], zt_sem.at[0])
    wait_all(qar, qa_sem.at[0])
    wait_all(agr.at[pl.ds(0, (nz - 1) * 8)], ag_sem.at[0])
    wait_all(pkr, pk_sem.at[1])
    total = pks[...]
    for n in range(7):
        total += pkr[n]
    scores_ref[...] = (
        total[0:4, 0:NT]
        / K
        * lax.rsqrt(total[0:4, 64 : 64 + NT] / K + EPSILON)
        * lax.rsqrt(total[4:8, 0:NT] / K + EPSILON)
    )
    wait_all(pkr, pk_sem.at[0])


def body(output_gradient, adapter_activations, proj, labels):
    nz, g = 16, GROUPS
    per = nz // g
    rw = per * 4
    proj = proj.reshape(proj.shape[0] * proj.shape[1], proj.shape[2])
    vm = pltpu.VMEM
    scratch = [
        vm((1024, 512), BF16),
        vm((1024, 64), BF16),
        vm((512, K), BF16),
        vm((4, 512, 128), F32),
        vm((1024, 128), F32),
        vm((nz, 4, 16, 128), BF16),
        vm((nz, 4, 16, 128), BF16),
        vm((nz, 4, 16, 128), BF16),
        vm((g, per * 64, 128), F32),
        vm((1, 128), jnp.int32),
        vm((nz, 1, 128), jnp.int32),
        vm((g, 4, 4, rw, 512), F32),
        vm((g, 4, 4, rw, 512), BF16),
        vm((g, 4, 4, rw, 512), BF16),
        vm((g, 4, rw, 256), F32),
        vm((g, 4, rw, 256), F32),
        vm((g, 3, 4, rw, 256), BF16),
        vm((g, 3, 4, rw, 256), BF16),
        vm((g, 3, 4, rw, 256), BF16),
        vm((g, 3, 4, rw, 256), BF16),
        vm((g, 3, rw, 256), F32),
        vm((g, 3, rw, 256), F32),
        vm((g, 3, rw, 256), F32),
        vm((g, 3, rw, 256), F32),
        vm((4, 4 * nz, 128), F32),
        vm((16 * nz, 128), F32),
        vm((nz, 16, 128), BF16),
        vm((nz, 16, 128), BF16),
        vm((4, NT, 128), F32),
        vm((8 * nz, 128), F32),
        vm((nz, 8, 128), F32),
        vm((2, 8, 128), F32),
        vm((3, 2, 8, 128), F32),
        vm((8 * nz, 128), F32),
        vm((8, 128), F32),
        vm((7, 8, 128), F32),
    ]
    dma = pltpu.SemaphoreType.DMA
    scratch += [
        dma((6,)),
        dma((2,)),
        dma((2,)),
        dma((2, 4)),
        dma(()),
        dma((g,)),
        dma((2, g)),
        dma((2, g)),
        dma((2, g)),
        dma((2, g)),
        dma((2, g)),
        dma(()),
        dma(()),
        dma((2,)),
        dma((2,)),
        dma((2,)),
        dma((2,)),
    ]
    hbm = pl.BlockSpec(memory_space=pl.ANY)
    vmem = pl.BlockSpec(memory_space=pltpu.VMEM)
    return pl.pallas_call(
        kernel,
        out_shape=(
            jax.ShapeDtypeStruct((4, NT), F32),
            jax.ShapeDtypeStruct((NT, 512), F32),
        ),
        in_specs=[hbm, hbm, hbm, vmem],
        out_specs=(vmem, vmem),
        scratch_shapes=scratch,
        compiler_params=pltpu.CompilerParams(
            collective_id=0, has_side_effects=True, vmem_limit_bytes=48 * 1024 * 1024
        ),
    )(output_gradient, adapter_activations, proj, labels.reshape(1, 4))


def solution(mesh):
    placed = (P("dp", "param"), P("dp", None), P(("param", "dp"), None, None), P("dp"))
    return jax.shard_map(
        body,
        mesh=mesh,
        in_specs=placed,
        out_specs=(P("dp", None), P(None, "param")),
        check_vma=False,
    )
```

```python
import jax
import jax.numpy as jnp
from jax import lax
from jax.experimental import pallas as pl
from jax.experimental.pallas import tpu as pltpu
from jax.sharding import PartitionSpec as P

K = 4096
NT = 32
EPSILON = 1e-06
MESH = pl.DeviceIdType.MESH
F32 = jnp.float32
BF16 = jnp.bfloat16
HIGHEST = lax.Precision.HIGHEST

OFFSETS = (0, 1, 15, 2, 14, 3, 13, 4, 12, 5, 11, 6, 10, 7, 9, 8)
NZ = 16
GROUPS = 2
PER = NZ // GROUPS
RW = PER * 4


def flip(value, bits):
    for bit in (1, 2, 4):
        if bits & bit:
            value = value + bit - 2 * bit * ((value // bit) % 2)
    return value


def kernel(
    og_h, act_h, proj_h, lab_h, scores_ref, means_ref,
    og_v, act_v, proj_v, lab_v, g32, s32, qs, rb, f32s, ls, lr, lq, lqr,
    own, cs, cr, sx, rx, dsum, zs32, zs, zr, tpart, zts, ztr, agr, pks, pkr,
    in_sem, loc_sem, lab_sem, lq_sem, zg_send, zg_recv, core_sem, xy_sem,
    zs_sem, zt_sem, ag_sem, pk_sem,
):
    dp, param = lax.axis_index("dp"), lax.axis_index("param")
    z, q = dp // 4, dp % 4
    xl, y = param // 4, param % 4

    def ahead(i, s=0):
        return ((z + OFFSETS[i]) % NZ) * 4 + flip(q, s)

    def behind(i, s=0):
        return ((z + NZ - OFFSETS[i]) % NZ) * 4 + flip(q, s)

    def plane_peer(n):
        return (flip(dp, (n // 8) * 2), flip(param, n % 8))

    def remote(src, dst, send, recv, device):
        return pltpu.make_async_remote_copy(
            src_ref=src, dst_ref=dst, send_sem=send, recv_sem=recv,
            device_id=device, device_id_type=MESH,
        )

    def wait_all(ref, sem):
        pltpu.make_async_copy(ref, ref, sem).wait()

    barrier = pltpu.get_barrier_semaphore()
    peers = [(ahead(i, s), param) for i in reversed(range(NZ)) for s in range(4) if i or s]
    peers += [plane_peer(n) for n in range(1, 16) if n != 8]
    for peer in peers:
        pl.semaphore_signal(barrier, inc=1, device_id=peer, device_id_type=MESH)

    act_in = pltpu.make_async_copy(act_h, act_v, in_sem.at[0])
    act_in.start()
    lab_in = pltpu.make_async_copy(lab_h, lab_v, in_sem.at[6])
    lab_in.start()
    og_in = []
    for m in range(4):
        copy = pltpu.make_async_copy(
            og_h.at[pl.ds(m * 256, 256)], og_v.at[pl.ds(m * 256, 256)], in_sem.at[2 + m]
        )
        copy.start()
        og_in.append(copy)
    proj_in = pltpu.make_async_copy(proj_h, proj_v, in_sem.at[1])
    proj_in.start()

    act_in.wait()
    low = lax.broadcasted_iota(jnp.int32, (64, 128), 1) < 64
    for m in range(4):
        og_in[m].wait()
        act = act_v[:, m * 256 : (m + 1) * 256]
        g32[m] = lax.dot_general(
            og_v[m * 256 : (m + 1) * 256, :],
            jnp.concatenate([act, act], axis=0),
            (((0,), (1,)), ((), ())),
            preferred_element_type=F32,
        )
        for j in range(4):
            even = g32[m, pl.ds(2 * j, 64, stride=8), :]
            odd = g32[m, pl.ds(2 * j + 1, 64, stride=8), :]
            s32[pl.ds(m * 4 + j, 64, stride=16), :] = jnp.where(low, even, odd)
    for block in range(NZ):
        qs[block * 4 : block * 4 + 4] = (
            s32[block * 64 : (block + 1) * 64, :].astype(BF16).reshape(4, 16, 128)
        )
    lab_in.wait()
    lane = lax.broadcasted_iota(jnp.int32, (1, 128), 1)
    label_row = jnp.zeros((1, 128), jnp.int32)
    for m in range(4):
        label_row = jnp.where(lane % 4 == m, lab_v[0:1, m : m + 1], label_row)
    ls[...] = label_row

    pl.semaphore_wait(barrier, len(peers))

    for i in range(NZ):
        for s in range(4):
            if i or s:
                remote(
                    qs.at[ahead(i, s)], rb.at[i * 4 + s], zg_send, zg_recv.at[i // PER], (ahead(i, s), param)
                ).start()
        if i:
            remote(ls, lr.at[i], lab_sem.at[0], lab_sem.at[1], (ahead(i), param)).start()
    lr[0] = label_row
    home = pltpu.make_async_copy(qs.at[dp], rb.at[0], loc_sem)
    home.start()
    home.wait()
    proj_in.wait()

    def project(c):
        first = max(1, c * PER * 4)
        wait_all(rb.at[pl.ds(first, (c + 1) * PER * 4 - first)], zg_recv.at[c])
        for s in range(4):
            for k in range(PER):
                at = (s * PER + k) * 16
                f32s[c, at : at + 16, :] = rb[(c * PER + k) * 4 + s].astype(F32)
        rows = jnp.concatenate(
            [f32s[c, pl.ds(j, 4 * RW, stride=4), :].astype(BF16) for j in range(4)], axis=1
        )
        for n in range(8):
            part = jnp.dot(
                rows,
                proj_v[:, pl.ds(pl.multiple_of(flip(param, n) * 512, 512), 512)],
                preferred_element_type=F32,
            )
            for h in range(2):
                own[c, h * 8 + n] = part[2 * h * RW : (2 * h + 1) * RW]
                cs[c, h * 8 + n] = part[(2 * h + 1) * RW : (2 * h + 2) * RW].astype(BF16)
        remote(
            cs.at[c], cr.at[c], core_sem.at[0, c], core_sem.at[1, c], (flip(dp, 1), param)
        ).start()

    def after_core(c):
        wait_all(cr.at[c], core_sem.at[1, c])
        for n in range(16):
            total = own[c, n] + cr[c, n].astype(F32)
            if n:
                sx[c, n] = total.astype(BF16)
                remote(
                    sx.at[c, n], rx.at[c, n], xy_sem.at[0, c], xy_sem.at[1, c], plane_peer(n)
                ).start()
            else:
                own[c, 0] = total

    def after_plane(c):
        wait_all(rx.at[c, pl.ds(1, 15)], xy_sem.at[1, c])
        for j in range(4):
            columns = slice(j * 128, (j + 1) * 128)
            total = own[c, 0, :, columns]
            for n in range(1, 16):
                total += rx[c, n, :, columns].astype(F32)
            dsum[j, c * RW : (c + 1) * RW, :] = total

    def send_examples(c):
        base = c * PER * 16
        for j in range(4):
            for m in range(4):
                zs32[pl.ds(base + j * 4 + m, PER, stride=16), :] = dsum[
                    j, pl.ds(c * RW + m, PER, stride=4), :
                ]
        for k in range(PER):
            i = c * PER + k
            zs[i] = zs32[i * 16 : (i + 1) * 16, :].astype(BF16)
        for i in range(max(1, c * PER), (c + 1) * PER):
            remote(zs.at[i], zr.at[i], zs_sem.at[0], zs_sem.at[1], (behind(i), param)).start()

    for step in range(GROUPS + 2):
        if 0 <= step - 2 < GROUPS:
            after_plane(step - 2)
            if step - 2 < GROUPS - 1:
                send_examples(step - 2)
        if 0 <= step - 1 < GROUPS:
            after_core(step - 1)
            if step == GROUPS:
                wait_all(lr.at[pl.ds(1, NZ - 1)], lab_sem.at[1])
                labels = jnp.full((1, 128), -1, jnp.int32)
                for i in range(NZ):
                    labels = jnp.where(lane // 4 == i, lr[i], labels)
                lq[...] = labels
                for s in (1, 2, 3):
                    remote(lq, lqr.at[s - 1], lq_sem.at[0], lq_sem.at[1], (flip(dp, s), param)).start()
        if step < GROUPS:
            project(step)

    row = lax.broadcasted_iota(jnp.int32, (NT, 4 * NZ), 0)
    tag = row % 2
    for i in range(NZ):
        tag = jnp.where(row // 2 == i, row % 2 + 2 * (behind(i) // 4), tag)
    onehot = (tag == labels[:, : 4 * NZ]).astype(BF16)
    for j in range(4):
        values = dsum[j]
        high = values.astype(BF16)
        rest = (values - high.astype(F32)).astype(BF16)
        sums = jnp.dot(onehot, high, preferred_element_type=F32) + jnp.dot(
            onehot, rest, preferred_element_type=F32
        )
        for i in range(NZ):
            zts[i, j] = sums[2 * i : 2 * i + 2, :]
    for i in reversed(range(NZ)):
        for s in range(4):
            if i or s:
                remote(
                    zts.at[i, flip(q, s)], ztr.at[i * 4 + s], zt_sem.at[0], zt_sem.at[1], (behind(i, s), param)
                ).start()
    send_examples(GROUPS - 1)
    wait_all(ztr.at[pl.ds(1, 4 * NZ - 1)], zt_sem.at[1])
    agr[dp] = zts[0, q] + jnp.sum(ztr[1:], axis=0)
    for i in reversed(range(NZ)):
        for s in range(4):
            if i or s:
                remote(
                    agr.at[dp], agr.at[dp], ag_sem.at[0], ag_sem.at[1], (ahead(i, s), param)
                ).start()

    wait_all(zr.at[pl.ds(1, NZ - 1)], zs_sem.at[1])
    mine16 = zs32[0:16, :]
    for i in range(1, NZ):
        mine16 += zr[i].astype(F32)
    grad_sq = jnp.zeros((4, 128), F32)
    for j in range(4):
        grad_sq += mine16[j * 4 : (j + 1) * 4, :] * mine16[j * 4 : (j + 1) * 4, :]
    grad_sq = jnp.sum(grad_sq, axis=1, keepdims=True)
    wait_all(lqr, lq_sem.at[1])
    task = lax.broadcasted_iota(jnp.int32, (NT, 128), 0)
    counts = (task == labels).astype(F32)
    for s in range(3):
        counts += (task == lqr[s]).astype(F32)
    counts = jnp.maximum(jnp.sum(counts, axis=1, keepdims=True), 1.0)

    wait_all(agr.at[pl.ds(0, 4 * NZ - 1)], ag_sem.at[1])
    dots = jnp.zeros((4, NT), F32)
    mean_sq = jnp.zeros((4, NT), F32)
    ones = jnp.ones((4, 128), F32)
    contract = (((1,), (1,)), ((), ()))
    for j in range(4):
        for block in range(NZ):
            tpart[j, 2 * block : 2 * block + 2, :] = agr[block * 4 + j]
        means = tpart[j] / counts
        means_ref[:, j * 128 : (j + 1) * 128] = means
        part = mine16[j * 4 : (j + 1) * 4, :]
        dots += lax.dot_general(part, means, contract, precision=HIGHEST, preferred_element_type=F32)
        mean_sq += lax.dot_general(ones, means * means, contract, precision=HIGHEST, preferred_element_type=F32)
    pks[...] = jnp.zeros((8, 128), F32)
    pks[0:4, 0:NT] = dots
    pks[4:8, 0:NT] = mean_sq
    pks[0:4, 64:128] = jnp.broadcast_to(grad_sq, (4, 64))
    for n in range(1, 8):
        remote(pks, pkr.at[n - 1], pk_sem.at[0], pk_sem.at[1], (dp, flip(param, n))).start()
    wait_all(rb.at[pl.ds(1, 4 * NZ - 1)], zg_send)
    wait_all(lr.at[pl.ds(1, NZ - 1)], lab_sem.at[0])
    wait_all(lqr, lq_sem.at[0])
    for c in range(GROUPS):
        wait_all(cs.at[c], core_sem.at[0, c])
        wait_all(sx.at[c, pl.ds(1, 15)], xy_sem.at[0, c])
    wait_all(zs.at[pl.ds(1, NZ - 1)], zs_sem.at[0])
    wait_all(ztr.at[pl.ds(1, 4 * NZ - 1)], zt_sem.at[0])
    wait_all(agr.at[pl.ds(0, 4 * NZ - 1)], ag_sem.at[0])
    wait_all(pkr, pk_sem.at[1])
    total = pks[...]
    for n in range(7):
        total += pkr[n]
    scores_ref[...] = (
        total[0:4, 0:NT]
        / K
        * lax.rsqrt(total[0:4, 64 : 64 + NT] / K + EPSILON)
        * lax.rsqrt(total[4:8, 0:NT] / K + EPSILON)
    )
    wait_all(pkr, pk_sem.at[0])


def body(output_gradient, adapter_activations, proj, labels):
    proj = proj.reshape(proj.shape[0] * proj.shape[1], proj.shape[2])
    vm = pltpu.VMEM
    scratch = [
        vm((1024, 512), BF16),
        vm((64, 1024), BF16),
        vm((512, K), BF16),
        vm((1, 4), jnp.int32),
        vm((4, 512, 128), F32),
        vm((1024, 128), F32),
        vm((4 * NZ, 16, 128), BF16),
        vm((4 * NZ, 16, 128), BF16),
        vm((GROUPS, PER * 64, 128), F32),
        vm((1, 128), jnp.int32),
        vm((NZ, 1, 128), jnp.int32),
        vm((1, 128), jnp.int32),
        vm((3, 1, 128), jnp.int32),
        vm((GROUPS, 16, RW, 512), F32),
        vm((GROUPS, 16, RW, 512), BF16),
        vm((GROUPS, 16, RW, 512), BF16),
        vm((GROUPS, 16, RW, 512), BF16),
        vm((GROUPS, 16, RW, 512), BF16),
        vm((4, 4 * NZ, 128), F32),
        vm((16 * NZ, 128), F32),
        vm((NZ, 16, 128), BF16),
        vm((NZ, 16, 128), BF16),
        vm((4, NT, 128), F32),
        vm((NZ, 4, 2, 128), F32),
        vm((4 * NZ, 2, 128), F32),
        vm((4 * NZ, 2, 128), F32),
        vm((8, 128), F32),
        vm((7, 8, 128), F32),
    ]
    dma = pltpu.SemaphoreType.DMA
    scratch += [
        dma((7,)),
        dma(()),
        dma((2,)),
        dma((2,)),
        dma(()),
        dma((GROUPS,)),
        dma((2, GROUPS)),
        dma((2, GROUPS)),
        dma((2,)),
        dma((2,)),
        dma((2,)),
        dma((2,)),
    ]
    hbm = pl.BlockSpec(memory_space=pl.ANY)
    vmem = pl.BlockSpec(memory_space=pltpu.VMEM)
    return pl.pallas_call(
        kernel,
        out_shape=(
            jax.ShapeDtypeStruct((4, NT), F32),
            jax.ShapeDtypeStruct((NT, 512), F32),
        ),
        in_specs=[hbm, hbm, hbm, hbm],
        out_specs=(vmem, vmem),
        scratch_shapes=scratch,
        compiler_params=pltpu.CompilerParams(
            collective_id=0, has_side_effects=True, vmem_limit_bytes=63 * 1024 * 1024
        ),
    )(output_gradient, adapter_activations.T, proj, labels.reshape(1, 4))


def solution(mesh):
    placed = (P("dp", "param"), P("dp", None), P(("param", "dp"), None, None), P("dp"))
    return jax.shard_map(
        body,
        mesh=mesh,
        in_specs=placed,
        out_specs=(P("dp", None), P(None, "param")),
        check_vma=False,
    )
```

```python
import jax
import jax.numpy as jnp
from jax import lax
from jax.experimental import pallas as pl
from jax.experimental.pallas import tpu as pltpu
from jax.sharding import PartitionSpec as P

K = 4096
NT = 32
EPSILON = 1e-06
MESH = pl.DeviceIdType.MESH
F32 = jnp.float32
BF16 = jnp.bfloat16
HIGHEST = lax.Precision.HIGHEST

OFFSETS = (0, 1, 15, 2, 14, 3, 13, 4, 12, 5, 11, 6, 10, 7, 9, 8)
NZ = 16
GROUPS = 2
PER = NZ // GROUPS
RW = PER * 4


def flip(value, bits):
    for bit in (1, 2, 4):
        if bits & bit:
            value = value + bit - 2 * bit * ((value // bit) % 2)
    return value


def kernel(
    og_h, act_h, proj_h, lab_h, scores_ref, means_ref,
    og_v, act_v, proj_v, lab_v, g32, s32, qs, rb, f32s, ls, lr, lq, lqr,
    xs, own, cs, cr, sx, rx, dsum, zs32, zs, zr,
    town, tcs, tcr, tsx, trx, ztb, ztr, agr, tpart, pks, pkr,
    in_sem, loc_sem, lab_sem, lq_sem, zg_send, zg_recv, core_sem, xy_sem,
    zs_sem, tc_sem, ty_sem, zt_sem, ag_sem, pk_sem,
):
    dp, param = lax.axis_index("dp"), lax.axis_index("param")
    z, q = dp // 4, dp % 4
    xl, y = param // 4, param % 4

    def ahead(i, s=0):
        return ((z + OFFSETS[i]) % NZ) * 4 + flip(q, s)

    def behind(i, s=0):
        return ((z + NZ - OFFSETS[i]) % NZ) * 4 + flip(q, s)

    def plane_peer(n):
        return (flip(dp, (n // 8) * 2), flip(param, n % 8))

    def remote(src, dst, send, recv, device):
        return pltpu.make_async_remote_copy(
            src_ref=src, dst_ref=dst, send_sem=send, recv_sem=recv,
            device_id=device, device_id_type=MESH,
        )

    def wait_all(ref, sem):
        pltpu.make_async_copy(ref, ref, sem).wait()

    act_in = pltpu.make_async_copy(act_h, act_v, in_sem.at[0])
    act_in.start()
    lab_in = pltpu.make_async_copy(lab_h, lab_v, in_sem.at[6])
    lab_in.start()
    og_in = []
    for m in range(4):
        copy = pltpu.make_async_copy(
            og_h.at[pl.ds(m * 256, 256)], og_v.at[pl.ds(m * 256, 256)], in_sem.at[2 + m]
        )
        copy.start()
        og_in.append(copy)
    proj_in = pltpu.make_async_copy(proj_h, proj_v, in_sem.at[1])
    proj_in.start()

    barrier = pltpu.get_barrier_semaphore()
    far = [(ahead(i, s), param) for i in reversed(range(5, NZ)) for s in range(4)]
    near = [(ahead(i, s), param) for i in reversed(range(5)) for s in range(4) if i or s]
    near += [plane_peer(n) for n in range(1, 16) if n != 8]

    def greet(peers):
        for peer in peers:
            pl.semaphore_signal(barrier, inc=1, device_id=peer, device_id_type=MESH)

    greet(far)

    act_in.wait()
    low = lax.broadcasted_iota(jnp.int32, (64, 128), 1) < 64
    for m in range(4):
        og_in[m].wait()
        act = act_v[:, m * 256 : (m + 1) * 256]
        g32[m] = lax.dot_general(
            og_v[m * 256 : (m + 1) * 256, :],
            jnp.concatenate([act, act], axis=0),
            (((0,), (1,)), ((), ())),
            preferred_element_type=F32,
        )
        for j in range(4):
            even = g32[m, pl.ds(2 * j, 64, stride=8), :]
            odd = g32[m, pl.ds(2 * j + 1, 64, stride=8), :]
            s32[pl.ds(m * 4 + j, 64, stride=16), :] = jnp.where(low, even, odd)
        if m == 0:
            greet(near)
    for block in range(NZ):
        qs[block * 4 : block * 4 + 4] = (
            s32[block * 64 : (block + 1) * 64, :].astype(BF16).reshape(4, 16, 128)
        )
    lab_in.wait()
    lane = lax.broadcasted_iota(jnp.int32, (1, 128), 1)
    label_row = jnp.zeros((1, 128), jnp.int32)
    for m in range(4):
        label_row = jnp.where(lane % 4 == m, lab_v[0:1, m : m + 1], label_row)
    ls[...] = label_row

    pl.semaphore_wait(barrier, len(far) + len(near))

    for i in range(1, NZ):
        remote(ls, lr.at[i], lab_sem.at[0], lab_sem.at[1], (ahead(i), param)).start()
    for i in range(NZ):
        for s in range(4):
            if i or s:
                remote(
                    qs.at[ahead(i, s)], rb.at[i * 4 + s], zg_send, zg_recv.at[i // PER], (ahead(i, s), param)
                ).start()
    lr[0] = label_row
    home = pltpu.make_async_copy(qs.at[dp], rb.at[0], loc_sem)
    home.start()
    home.wait()
    proj_in.wait()

    def arrange(c):
        first = max(1, c * PER * 4)
        wait_all(rb.at[pl.ds(first, (c + 1) * PER * 4 - first)], zg_recv.at[c])
        for s in range(4):
            for k in range(PER):
                at = (s * PER + k) * 16
                f32s[c, at : at + 16, :] = rb[(c * PER + k) * 4 + s].astype(F32)
        rows = jnp.concatenate(
            [f32s[c, pl.ds(j, 4 * RW, stride=4), :].astype(BF16) for j in range(4)], axis=1
        )
        xs[c] = rows

    def projected(rows, n):
        columns = pl.ds(pl.multiple_of(flip(param, n) * 512, 512), 512)
        return jnp.dot(rows, proj_v[:, columns], preferred_element_type=F32)

    def project(c):
        rows = xs[c]
        for n in range(8):
            part = projected(rows, n)
            for h in range(2):
                own[c, h * 8 + n] = part[2 * h * RW : (2 * h + 1) * RW]
                cs[c, h * 8 + n] = part[(2 * h + 1) * RW : (2 * h + 2) * RW].astype(BF16)
        remote(
            cs.at[c], cr.at[c], core_sem.at[0, c], core_sem.at[1, c], (flip(dp, 1), param)
        ).start()

    def after_core(c):
        wait_all(cr.at[c], core_sem.at[1, c])
        for n in range(16):
            total = own[c, n] + cr[c, n].astype(F32)
            if n:
                sx[c, n] = total.astype(BF16)
                remote(
                    sx.at[c, n], rx.at[c, n], xy_sem.at[0, c], xy_sem.at[1, c], plane_peer(n)
                ).start()
            else:
                own[c, 0] = total

    def after_plane(c):
        wait_all(rx.at[c, pl.ds(1, 15)], xy_sem.at[1, c])
        for j in range(4):
            columns = slice(j * 128, (j + 1) * 128)
            total = own[c, 0, :, columns]
            for n in range(1, 16):
                total += rx[c, n, :, columns].astype(F32)
            dsum[j, c * RW : (c + 1) * RW, :] = total

    def send_examples(c):
        base = c * PER * 16
        for j in range(4):
            for m in range(4):
                zs32[pl.ds(base + j * 4 + m, PER, stride=16), :] = dsum[
                    j, pl.ds(c * RW + m, PER, stride=4), :
                ]
        for k in range(PER):
            i = c * PER + k
            zs[i] = zs32[i * 16 : (i + 1) * 16, :].astype(BF16)
        for i in range(max(1, c * PER), (c + 1) * PER):
            remote(zs.at[i], zr.at[i], zs_sem.at[0], zs_sem.at[1], (behind(i), param)).start()

    for c in range(GROUPS - 1):
        arrange(c)
        project(c)
        if c:
            after_core(c - 1)

    wait_all(lr.at[pl.ds(1, NZ - 1)], lab_sem.at[1])
    labels = jnp.full((1, 128), -1, jnp.int32)
    for i in range(NZ):
        labels = jnp.where(lane // 4 == i, lr[i], labels)
    lq[...] = labels
    for s in (1, 2, 3):
        remote(lq, lqr.at[s - 1], lq_sem.at[0], lq_sem.at[1], (flip(dp, s), param)).start()
    if GROUPS > 1:
        after_core(GROUPS - 2)
    wait_all(lqr, lq_sem.at[1])

    arrange(GROUPS - 1)
    row = lax.broadcasted_iota(jnp.int32, (NT, 4 * NZ), 0)
    tag = row % 8
    for s in range(4):
        tag = jnp.where(row // 8 == s, row % 8 + 8 * flip(q, s), tag)
    sums = jnp.zeros((NT, 512), F32)
    for s in range(4):
        known = labels if s == 0 else lqr[s - 1]
        onehot = (tag == known[:, : 4 * NZ]).astype(BF16)
        rows = jnp.concatenate([xs[c, s * RW : (s + 1) * RW, :] for c in range(GROUPS)], axis=0)
        sums += jnp.dot(onehot, rows, preferred_element_type=F32)
    high = sums.astype(BF16)
    parts = jnp.concatenate([high, (sums - high.astype(F32)).astype(BF16)], axis=0)
    for n in range(8):
        part = projected(parts, n)
        part = part[:NT] + part[NT:]
        for h in range(2):
            town[h * 8 + n] = part[16 * h : 16 * h + 8]
            tcs[h * 8 + n] = part[16 * h + 8 : 16 * h + 16]
    remote(tcs, tcr, tc_sem.at[0], tc_sem.at[1], (flip(dp, 1), param)).start()
    project(GROUPS - 1)

    def stacked(value):
        return jnp.concatenate([value[:, :256], value[:, 256:]], axis=0)

    wait_all(tcr, tc_sem.at[1])
    for n in range(1, 16):
        tsx[n] = stacked(town[n] + tcr[n]).astype(BF16)
        remote(tsx.at[n], trx.at[n], ty_sem.at[0], ty_sem.at[1], plane_peer(n)).start()
    label_sums = stacked(town[0] + tcr[0])
    after_core(GROUPS - 1)
    for c in range(GROUPS - 1):
        after_plane(c)
        send_examples(c)

    wait_all(trx.at[pl.ds(1, 15)], ty_sem.at[1])
    for n in range(1, 16):
        label_sums += trx[n].astype(F32)
    for n in range(NZ):
        ztb[n] = label_sums[n : n + 1, :]
    for i in reversed(range(1, NZ)):
        remote(
            ztb.at[behind(i) // 4], ztr.at[i], zt_sem.at[0], zt_sem.at[1], (behind(i), param)
        ).start()
    after_plane(GROUPS - 1)
    send_examples(GROUPS - 1)
    wait_all(ztr.at[pl.ds(1, NZ - 1)], zt_sem.at[1])
    total = ztb[z]
    for i in range(1, NZ):
        total += ztr[i]
    agr[dp] = total
    for i in reversed(range(NZ)):
        for s in range(4):
            if i or s:
                remote(
                    agr.at[dp], agr.at[dp], ag_sem.at[0], ag_sem.at[1], (ahead(i, s), param)
                ).start()

    wait_all(zr.at[pl.ds(1, NZ - 1)], zs_sem.at[1])
    mine16 = zs32[0:16, :]
    for i in range(1, NZ):
        mine16 += zr[i].astype(F32)
    grad_sq = jnp.zeros((4, 128), F32)
    for j in range(4):
        grad_sq += mine16[j * 4 : (j + 1) * 4, :] * mine16[j * 4 : (j + 1) * 4, :]
    grad_sq = jnp.sum(grad_sq, axis=1, keepdims=True)
    task = lax.broadcasted_iota(jnp.int32, (NT, 128), 0)
    counts = (task == labels).astype(F32)
    for s in range(3):
        counts += (task == lqr[s]).astype(F32)
    counts = jnp.maximum(jnp.sum(counts, axis=1, keepdims=True), 1.0)

    wait_all(agr.at[pl.ds(0, 4 * NZ - 1)], ag_sem.at[1])
    dots = jnp.zeros((4, NT), F32)
    mean_sq = jnp.zeros((4, NT), F32)
    ones = jnp.ones((4, 128), F32)
    contract = (((1,), (1,)), ((), ()))
    for n in range(NZ):
        for j in range(4):
            tpart[n // 8, 8 * j + n % 8 : 8 * j + n % 8 + 1, :] = agr[n * 4 + j]
    for j in range(4):
        means = tpart[j // 2, :, (j % 2) * 128 : (j % 2 + 1) * 128] / counts
        means_ref[:, j * 128 : (j + 1) * 128] = means
        part = mine16[j * 4 : (j + 1) * 4, :]
        dots += lax.dot_general(part, means, contract, precision=HIGHEST, preferred_element_type=F32)
        mean_sq += lax.dot_general(ones, means * means, contract, precision=HIGHEST, preferred_element_type=F32)
    pks[...] = jnp.zeros((8, 128), F32)
    pks[0:4, 0:NT] = dots
    pks[4:8, 0:NT] = mean_sq
    pks[0:4, 64:128] = jnp.broadcast_to(grad_sq, (4, 64))
    for n in range(1, 8):
        remote(pks, pkr.at[n - 1], pk_sem.at[0], pk_sem.at[1], (dp, flip(param, n))).start()
    wait_all(rb.at[pl.ds(1, 4 * NZ - 1)], zg_send)
    wait_all(lr.at[pl.ds(1, NZ - 1)], lab_sem.at[0])
    wait_all(lqr, lq_sem.at[0])
    for c in range(GROUPS):
        wait_all(cs.at[c], core_sem.at[0, c])
        wait_all(sx.at[c, pl.ds(1, 15)], xy_sem.at[0, c])
    wait_all(zs.at[pl.ds(1, NZ - 1)], zs_sem.at[0])
    wait_all(tcs, tc_sem.at[0])
    wait_all(tsx.at[pl.ds(1, 15)], ty_sem.at[0])
    wait_all(ztr.at[pl.ds(1, NZ - 1)], zt_sem.at[0])
    wait_all(agr.at[pl.ds(0, 4 * NZ - 1)], ag_sem.at[0])
    wait_all(pkr, pk_sem.at[1])
    total = pks[...]
    for n in range(7):
        total += pkr[n]
    scores_ref[...] = (
        total[0:4, 0:NT]
        / K
        * lax.rsqrt(total[0:4, 64 : 64 + NT] / K + EPSILON)
        * lax.rsqrt(total[4:8, 0:NT] / K + EPSILON)
    )
    wait_all(pkr, pk_sem.at[0])


def body(output_gradient, adapter_activations, proj, labels):
    proj = proj.reshape(proj.shape[0] * proj.shape[1], proj.shape[2])
    vm = pltpu.VMEM
    scratch = [
        vm((1024, 512), BF16),
        vm((64, 1024), BF16),
        vm((512, K), BF16),
        vm((1, 4), jnp.int32),
        vm((4, 512, 128), F32),
        vm((1024, 128), F32),
        vm((4 * NZ, 16, 128), BF16),
        vm((4 * NZ, 16, 128), BF16),
        vm((GROUPS, PER * 64, 128), F32),
        vm((1, 128), jnp.int32),
        vm((NZ, 1, 128), jnp.int32),
        vm((1, 128), jnp.int32),
        vm((3, 1, 128), jnp.int32),
        vm((GROUPS, 4 * RW, 512), BF16),
        vm((GROUPS, 16, RW, 512), F32),
        vm((GROUPS, 16, RW, 512), BF16),
        vm((GROUPS, 16, RW, 512), BF16),
        vm((GROUPS, 16, RW, 512), BF16),
        vm((GROUPS, 16, RW, 512), BF16),
        vm((4, 4 * NZ, 128), F32),
        vm((16 * NZ, 128), F32),
        vm((NZ, 16, 128), BF16),
        vm((NZ, 16, 128), BF16),
        vm((16, 8, 512), F32),
        vm((16, 8, 512), F32),
        vm((16, 8, 512), F32),
        vm((16, 16, 256), BF16),
        vm((16, 16, 256), BF16),
        vm((NZ, 1, 256), F32),
        vm((NZ, 1, 256), F32),
        vm((4 * NZ, 1, 256), F32),
        vm((2, NT, 256), F32),
        vm((8, 128), F32),
        vm((7, 8, 128), F32),
    ]
    dma = pltpu.SemaphoreType.DMA
    scratch += [
        dma((7,)),
        dma(()),
        dma((2,)),
        dma((2,)),
        dma(()),
        dma((GROUPS,)),
        dma((2, GROUPS)),
        dma((2, GROUPS)),
        dma((2,)),
        dma((2,)),
        dma((2,)),
        dma((2,)),
        dma((2,)),
        dma((2,)),
    ]
    hbm = pl.BlockSpec(memory_space=pl.ANY)
    vmem = pl.BlockSpec(memory_space=pltpu.VMEM)
    return pl.pallas_call(
        kernel,
        out_shape=(
            jax.ShapeDtypeStruct((4, NT), F32),
            jax.ShapeDtypeStruct((NT, 512), F32),
        ),
        in_specs=[hbm, hbm, hbm, hbm],
        out_specs=(vmem, vmem),
        scratch_shapes=scratch,
        compiler_params=pltpu.CompilerParams(
            collective_id=0, has_side_effects=True, vmem_limit_bytes=63 * 1024 * 1024
        ),
    )(output_gradient, adapter_activations.T, proj, labels.reshape(1, 4))


def solution(mesh):
    placed = (P("dp", "param"), P("dp", None), P(("param", "dp"), None, None), P("dp"))
    return jax.shard_map(
        body,
        mesh=mesh,
        in_specs=placed,
        out_specs=(P("dp", None), P(None, "param")),
        check_vma=False,
    )
```

```python
import jax
import jax.numpy as jnp
from jax import lax
from jax.experimental import pallas as pl
from jax.experimental.pallas import tpu as pltpu
from jax.sharding import PartitionSpec as P

K = 4096
NT = 32
EPSILON = 1e-06
MESH = pl.DeviceIdType.MESH
F32 = jnp.float32
BF16 = jnp.bfloat16
HIGHEST = lax.Precision.HIGHEST

OFFSETS = (0, 1, 15, 2, 14, 3, 13, 4, 12, 5, 11, 6, 10, 7, 9, 8)
NZ = 16
GROUPS = 2
PER = NZ // GROUPS
RW = PER * 4


def flip(value, bits):
    for bit in (1, 2, 4):
        if bits & bit:
            value = value + bit - 2 * bit * ((value // bit) % 2)
    return value


def kernel(
    og_h, act_h, proj_h, lab_h, scores_ref, means_ref,
    og_v, act_v, proj_v, lab_v, g32, s32, qs, rb, f32s, ls, lr, lq, lqr,
    xs, own, cs, cr, sx, rx, dsum, zs32, zs, zr,
    town, tcs, tcr, tsx, trx, ztb, ztr, agr, pks, pkr,
    in_sem, loc_sem, lab_sem, lq_sem, zg_send, zg_recv, core_sem, xy_sem,
    zs_sem, tc_sem, ty_sem, zt_sem, ag_sem, pk_sem,
):
    dp, param = lax.axis_index("dp"), lax.axis_index("param")
    z, q = dp // 4, dp % 4
    xl, y = param // 4, param % 4

    def ahead(i, s=0):
        return ((z + OFFSETS[i]) % NZ) * 4 + flip(q, s)

    def behind(i, s=0):
        return ((z + NZ - OFFSETS[i]) % NZ) * 4 + flip(q, s)

    def plane_peer(n):
        return (flip(dp, (n // 8) * 2), flip(param, n % 8))

    def remote(src, dst, send, recv, device):
        return pltpu.make_async_remote_copy(
            src_ref=src, dst_ref=dst, send_sem=send, recv_sem=recv,
            device_id=device, device_id_type=MESH,
        )

    def wait_all(ref, sem):
        pltpu.make_async_copy(ref, ref, sem).wait()

    act_in = pltpu.make_async_copy(act_h, act_v, in_sem.at[0])
    act_in.start()
    lab_in = pltpu.make_async_copy(lab_h, lab_v, in_sem.at[6])
    lab_in.start()
    og_in = []
    for m in range(4):
        copy = pltpu.make_async_copy(
            og_h.at[pl.ds(m * 256, 256)], og_v.at[pl.ds(m * 256, 256)], in_sem.at[2 + m]
        )
        copy.start()
        og_in.append(copy)
    proj_in = pltpu.make_async_copy(proj_h, proj_v, in_sem.at[1])
    proj_in.start()

    barrier = pltpu.get_barrier_semaphore()
    far = [(ahead(i, s), param) for i in reversed(range(5, NZ)) for s in range(4)]
    near = [(ahead(i, s), param) for i in reversed(range(5)) for s in range(4) if i or s]
    near += [plane_peer(n) for n in range(1, 16) if n != 8]

    def greet(peers):
        for peer in peers:
            pl.semaphore_signal(barrier, inc=1, device_id=peer, device_id_type=MESH)

    greet(far)

    act_in.wait()
    low = lax.broadcasted_iota(jnp.int32, (64, 128), 1) < 64
    for m in range(4):
        og_in[m].wait()
        act = act_v[:, m * 256 : (m + 1) * 256]
        g32[m] = lax.dot_general(
            og_v[m * 256 : (m + 1) * 256, :],
            jnp.concatenate([act, act], axis=0),
            (((0,), (1,)), ((), ())),
            preferred_element_type=F32,
        )
        for j in range(4):
            even = g32[m, pl.ds(2 * j, 64, stride=8), :]
            odd = g32[m, pl.ds(2 * j + 1, 64, stride=8), :]
            s32[pl.ds(m * 4 + j, 64, stride=16), :] = jnp.where(low, even, odd)
        if m == 0:
            greet(near)
    for block in range(NZ):
        qs[block * 4 : block * 4 + 4] = (
            s32[block * 64 : (block + 1) * 64, :].astype(BF16).reshape(4, 16, 128)
        )
    lab_in.wait()
    lane = lax.broadcasted_iota(jnp.int32, (1, 128), 1)
    label_row = jnp.zeros((1, 128), jnp.int32)
    for m in range(4):
        label_row = jnp.where(lane % 4 == m, lab_v[0:1, m : m + 1], label_row)
    ls[...] = label_row

    pl.semaphore_wait(barrier, len(far) + len(near))

    for i in range(1, NZ):
        remote(ls, lr.at[i], lab_sem.at[0], lab_sem.at[1], (ahead(i), param)).start()
    for i in range(NZ):
        for s in range(4):
            if i or s:
                remote(
                    qs.at[ahead(i, s)], rb.at[i * 4 + s], zg_send, zg_recv.at[i // PER], (ahead(i, s), param)
                ).start()
    lr[0] = label_row
    home = pltpu.make_async_copy(qs.at[dp], rb.at[0], loc_sem)
    home.start()
    home.wait()
    proj_in.wait()

    def arrange(c):
        first = max(1, c * PER * 4)
        wait_all(rb.at[pl.ds(first, (c + 1) * PER * 4 - first)], zg_recv.at[c])
        for s in range(4):
            for k in range(PER):
                at = (s * PER + k) * 16
                f32s[c, at : at + 16, :] = rb[(c * PER + k) * 4 + s].astype(F32)
        rows = jnp.concatenate(
            [f32s[c, pl.ds(j, 4 * RW, stride=4), :].astype(BF16) for j in range(4)], axis=1
        )
        xs[c] = rows

    def projected(rows, n):
        columns = pl.ds(pl.multiple_of(flip(param, n) * 512, 512), 512)
        return jnp.dot(rows, proj_v[:, columns], preferred_element_type=F32)

    def project(c):
        rows = xs[c]
        for n in range(8):
            part = projected(rows, n)
            for h in range(2):
                own[c, h * 8 + n] = part[2 * h * RW : (2 * h + 1) * RW]
                cs[c, h * 8 + n] = part[(2 * h + 1) * RW : (2 * h + 2) * RW].astype(BF16)
        remote(
            cs.at[c], cr.at[c], core_sem.at[0, c], core_sem.at[1, c], (flip(dp, 1), param)
        ).start()

    def after_core(c):
        wait_all(cr.at[c], core_sem.at[1, c])
        for n in range(16):
            total = own[c, n] + cr[c, n].astype(F32)
            if n:
                sx[c, n] = total.astype(BF16)
                remote(
                    sx.at[c, n], rx.at[c, n], xy_sem.at[0, c], xy_sem.at[1, c], plane_peer(n)
                ).start()
            else:
                own[c, 0] = total

    def after_plane(c):
        wait_all(rx.at[c, pl.ds(1, 15)], xy_sem.at[1, c])
        for j in range(4):
            columns = slice(j * 128, (j + 1) * 128)
            total = own[c, 0, :, columns]
            for n in range(1, 16):
                total += rx[c, n, :, columns].astype(F32)
            dsum[j, c * RW : (c + 1) * RW, :] = total

    def send_examples(c):
        base = c * PER * 16
        for j in range(4):
            for m in range(4):
                zs32[pl.ds(base + j * 4 + m, PER, stride=16), :] = dsum[
                    j, pl.ds(c * RW + m, PER, stride=4), :
                ]
        for k in range(PER):
            i = c * PER + k
            zs[i] = zs32[i * 16 : (i + 1) * 16, :].astype(BF16)
        for i in range(max(1, c * PER), (c + 1) * PER):
            remote(zs.at[i], zr.at[i], zs_sem.at[0], zs_sem.at[1], (behind(i), param)).start()

    for c in range(GROUPS - 1):
        arrange(c)
        project(c)
        if c:
            after_core(c - 1)

    wait_all(lr.at[pl.ds(1, NZ - 1)], lab_sem.at[1])
    labels = jnp.full((1, 128), -1, jnp.int32)
    for i in range(NZ):
        labels = jnp.where(lane // 4 == i, lr[i], labels)
    lq[...] = labels
    for s in (1, 2, 3):
        remote(lq, lqr.at[s - 1], lq_sem.at[0], lq_sem.at[1], (flip(dp, s), param)).start()
    if GROUPS > 1:
        after_core(GROUPS - 2)
    wait_all(lqr, lq_sem.at[1])

    arrange(GROUPS - 1)
    row = lax.broadcasted_iota(jnp.int32, (NT, 4 * NZ), 0)
    tag = row % 8
    for s in range(4):
        tag = jnp.where(row // 8 == s, row % 8 + 8 * flip(q, s), tag)
    sums = jnp.zeros((NT, 512), F32)
    for s in range(4):
        known = labels if s == 0 else lqr[s - 1]
        onehot = (tag == known[:, : 4 * NZ]).astype(BF16)
        rows = jnp.concatenate([xs[c, s * RW : (s + 1) * RW, :] for c in range(GROUPS)], axis=0)
        sums += jnp.dot(onehot, rows, preferred_element_type=F32)
    high = sums.astype(BF16)
    parts = jnp.concatenate([high, (sums - high.astype(F32)).astype(BF16)], axis=0)
    for n in range(8):
        part = projected(parts, n)
        part = part[:NT] + part[NT:]
        for h in range(2):
            town[h * 8 + n] = part[16 * h : 16 * h + 8]
            tcs[h * 8 + n] = part[16 * h + 8 : 16 * h + 16]
    remote(tcs, tcr, tc_sem.at[0], tc_sem.at[1], (flip(dp, 1), param)).start()
    project(GROUPS - 1)

    def stacked(value):
        return jnp.concatenate([value[:, :256], value[:, 256:]], axis=0)

    wait_all(tcr, tc_sem.at[1])
    for n in range(1, 16):
        tsx[n] = stacked(town[n] + tcr[n]).astype(BF16)
        remote(tsx.at[n], trx.at[n], ty_sem.at[0], ty_sem.at[1], plane_peer(n)).start()
    label_sums = stacked(town[0] + tcr[0])
    after_core(GROUPS - 1)
    for c in range(GROUPS - 1):
        after_plane(c)
        send_examples(c)

    wait_all(trx.at[pl.ds(1, 15)], ty_sem.at[1])
    for n in range(1, 16):
        label_sums += trx[n].astype(F32)
    ztb[...] = label_sums.astype(BF16)
    for i in reversed(range(1, NZ)):
        remote(ztb, ztr.at[i], zt_sem.at[0], zt_sem.at[1], (ahead(i), param)).start()
    after_plane(GROUPS - 1)
    send_examples(GROUPS - 1)
    wait_all(ztr.at[pl.ds(1, NZ - 1)], zt_sem.at[1])
    for i in range(1, NZ):
        label_sums += ztr[i].astype(F32)
    agr[q] = jnp.concatenate([label_sums[:8], label_sums[8:]], axis=1)
    for s in (2, 3, 1):
        remote(agr.at[q], agr.at[q], ag_sem.at[0], ag_sem.at[1], (flip(dp, s), param)).start()

    wait_all(zr.at[pl.ds(1, NZ - 1)], zs_sem.at[1])
    mine16 = zs32[0:16, :]
    for i in range(1, NZ):
        mine16 += zr[i].astype(F32)
    mine = jnp.concatenate([mine16[j * 4 : (j + 1) * 4, :] for j in range(4)], axis=1)
    mine = jnp.concatenate([mine, jnp.zeros((4, 512), F32)], axis=0)
    grad_sq = jnp.sum(mine * mine, axis=1, keepdims=True)
    task = lax.broadcasted_iota(jnp.int32, (NT, 128), 0)
    counts = (task == labels).astype(F32)
    for s in range(3):
        counts += (task == lqr[s]).astype(F32)
    counts = jnp.maximum(jnp.sum(counts, axis=1, keepdims=True), 1.0)

    wait_all(agr.at[pl.ds(0, 3)], ag_sem.at[1])
    means = agr[...].reshape(NT, 512) / counts
    means_ref[...] = means
    contract = (((1,), (1,)), ((), ()))
    dots = lax.dot_general(mine, means, contract, precision=HIGHEST, preferred_element_type=F32)
    mean_sq = lax.dot_general(
        jnp.ones((8, 512), F32), means * means, contract, precision=HIGHEST, preferred_element_type=F32
    )
    pks[:, 0:64] = jnp.concatenate([dots, mean_sq], axis=1)
    pks[:, 64:128] = jnp.broadcast_to(grad_sq, (8, 64))
    for n in range(1, 8):
        remote(pks, pkr.at[n - 1], pk_sem.at[0], pk_sem.at[1], (dp, flip(param, n))).start()
    wait_all(rb.at[pl.ds(1, 4 * NZ - 1)], zg_send)
    wait_all(lr.at[pl.ds(1, NZ - 1)], lab_sem.at[0])
    wait_all(lqr, lq_sem.at[0])
    for c in range(GROUPS):
        wait_all(cs.at[c], core_sem.at[0, c])
        wait_all(sx.at[c, pl.ds(1, 15)], xy_sem.at[0, c])
    wait_all(zs.at[pl.ds(1, NZ - 1)], zs_sem.at[0])
    wait_all(tcs, tc_sem.at[0])
    wait_all(tsx.at[pl.ds(1, 15)], ty_sem.at[0])
    wait_all(ztr.at[pl.ds(1, NZ - 1)], zt_sem.at[0])
    wait_all(agr.at[pl.ds(0, 3)], ag_sem.at[0])
    wait_all(pkr, pk_sem.at[1])
    total = pks[...]
    for n in range(7):
        total += pkr[n]
    scores_ref[...] = (
        total[0:4, 0:NT]
        / K
        * lax.rsqrt(total[0:4, 64 : 64 + NT] / K + EPSILON)
        * lax.rsqrt(total[0:4, NT : 2 * NT] / K + EPSILON)
    )
    wait_all(pkr, pk_sem.at[0])


def body(output_gradient, adapter_activations, proj, labels):
    proj = proj.reshape(proj.shape[0] * proj.shape[1], proj.shape[2])
    vm = pltpu.VMEM
    scratch = [
        vm((1024, 512), BF16),
        vm((64, 1024), BF16),
        vm((512, K), BF16),
        vm((1, 4), jnp.int32),
        vm((4, 512, 128), F32),
        vm((1024, 128), F32),
        vm((4 * NZ, 16, 128), BF16),
        vm((4 * NZ, 16, 128), BF16),
        vm((GROUPS, PER * 64, 128), F32),
        vm((1, 128), jnp.int32),
        vm((NZ, 1, 128), jnp.int32),
        vm((1, 128), jnp.int32),
        vm((3, 1, 128), jnp.int32),
        vm((GROUPS, 4 * RW, 512), BF16),
        vm((GROUPS, 16, RW, 512), F32),
        vm((GROUPS, 16, RW, 512), BF16),
        vm((GROUPS, 16, RW, 512), BF16),
        vm((GROUPS, 16, RW, 512), BF16),
        vm((GROUPS, 16, RW, 512), BF16),
        vm((4, 4 * NZ, 128), F32),
        vm((16 * NZ, 128), F32),
        vm((NZ, 16, 128), BF16),
        vm((NZ, 16, 128), BF16),
        vm((16, 8, 512), F32),
        vm((16, 8, 512), F32),
        vm((16, 8, 512), F32),
        vm((16, 16, 256), BF16),
        vm((16, 16, 256), BF16),
        vm((16, 256), BF16),
        vm((NZ, 16, 256), BF16),
        vm((4, 8, 512), F32),
        vm((8, 128), F32),
        vm((7, 8, 128), F32),
    ]
    dma = pltpu.SemaphoreType.DMA
    scratch += [
        dma((7,)),
        dma(()),
        dma((2,)),
        dma((2,)),
        dma(()),
        dma((GROUPS,)),
        dma((2, GROUPS)),
        dma((2, GROUPS)),
        dma((2,)),
        dma((2,)),
        dma((2,)),
        dma((2,)),
        dma((2,)),
        dma((2,)),
    ]
    hbm = pl.BlockSpec(memory_space=pl.ANY)
    vmem = pl.BlockSpec(memory_space=pltpu.VMEM)
    return pl.pallas_call(
        kernel,
        out_shape=(
            jax.ShapeDtypeStruct((4, NT), F32),
            jax.ShapeDtypeStruct((NT, 512), F32),
        ),
        in_specs=[hbm, hbm, hbm, hbm],
        out_specs=(vmem, vmem),
        scratch_shapes=scratch,
        compiler_params=pltpu.CompilerParams(
            collective_id=0, has_side_effects=True, vmem_limit_bytes=63 * 1024 * 1024
        ),
    )(output_gradient, adapter_activations.T, proj, labels.reshape(1, 4))


def solution(mesh):
    placed = (P("dp", "param"), P("dp", None), P(("param", "dp"), None, None), P("dp"))
    return jax.shard_map(
        body,
        mesh=mesh,
        in_specs=placed,
        out_specs=(P("dp", None), P(None, "param")),
        check_vma=False,
    )
```

```python
import jax
import jax.numpy as jnp
from jax import lax
from jax.experimental import pallas as pl
from jax.experimental.pallas import tpu as pltpu
from jax.sharding import PartitionSpec as P

K = 4096
NT = 32
EPSILON = 1e-06
MESH = pl.DeviceIdType.MESH
F32 = jnp.float32
BF16 = jnp.bfloat16
HIGHEST = lax.Precision.HIGHEST

OFFSETS = (0, 1, 15, 2, 14, 3, 13, 4, 12, 5, 11, 6, 10, 7, 9, 8)
NZ = 16
GROUPS = 2
PER = NZ // GROUPS
RW = PER * 4


def flip(value, bits):
    for bit in (1, 2, 4):
        if bits & bit:
            value = value + bit - 2 * bit * ((value // bit) % 2)
    return value


def kernel(
    og_h, act_h, proj_h, lab_h, scores_ref, means_ref,
    og_v, act_v, proj_v, lab_v, g32, s32, qs, rb, f32s, ls, lr, lq, lqr,
    xs, own, cs, cr, sx, rx, dsum, zs32, zs, zr,
    town, tcs, tcr, tsx, trx, ztb, ztr, agr, pks, pkr,
    in_sem, loc_sem, lab_sem, lq_sem, zg_send, zg_recv, core_sem, xy_sem,
    zs_sem, tc_sem, ty_sem, zt_sem, ag_sem, pk_sem,
):
    dp, param = lax.axis_index("dp"), lax.axis_index("param")
    z, q = dp // 4, dp % 4
    xl, y = param // 4, param % 4

    def ahead(i, s=0):
        return ((z + OFFSETS[i]) % NZ) * 4 + flip(q, s)

    def behind(i, s=0):
        return ((z + NZ - OFFSETS[i]) % NZ) * 4 + flip(q, s)

    def plane_peer(n):
        return (flip(dp, (n // 8) * 2), flip(param, n % 8))

    def remote(src, dst, send, recv, device):
        return pltpu.make_async_remote_copy(
            src_ref=src, dst_ref=dst, send_sem=send, recv_sem=recv,
            device_id=device, device_id_type=MESH,
        )

    def wait_all(ref, sem):
        pltpu.make_async_copy(ref, ref, sem).wait()

    act_in = pltpu.make_async_copy(act_h, act_v, in_sem.at[0])
    act_in.start()
    lab_in = pltpu.make_async_copy(lab_h, lab_v, in_sem.at[6])
    lab_in.start()
    og_in = []
    for m in range(4):
        copy = pltpu.make_async_copy(
            og_h.at[pl.ds(m * 256, 256)], og_v.at[pl.ds(m * 256, 256)], in_sem.at[2 + m]
        )
        copy.start()
        og_in.append(copy)
    proj_in = pltpu.make_async_copy(proj_h, proj_v, in_sem.at[1])
    proj_in.start()

    barrier = pltpu.get_barrier_semaphore()
    far = [(ahead(i, s), param) for i in reversed(range(5, NZ)) for s in range(4)]
    near = [(ahead(i, s), param) for i in reversed(range(5)) for s in range(4) if i or s]
    near += [plane_peer(n) for n in range(1, 16) if n != 8]

    def greet(peers):
        for peer in peers:
            pl.semaphore_signal(barrier, inc=1, device_id=peer, device_id_type=MESH)

    greet(far)

    act_in.wait()
    low = lax.broadcasted_iota(jnp.int32, (64, 128), 1) < 64
    for m in range(4):
        og_in[m].wait()
        act = act_v[:, m * 256 : (m + 1) * 256]
        g32[m] = lax.dot_general(
            og_v[m * 256 : (m + 1) * 256, :],
            jnp.concatenate([act, act], axis=0),
            (((0,), (1,)), ((), ())),
            preferred_element_type=F32,
        )
        for j in range(4):
            even = g32[m, pl.ds(2 * j, 64, stride=8), :]
            odd = g32[m, pl.ds(2 * j + 1, 64, stride=8), :]
            s32[pl.ds(m * 4 + j, 64, stride=16), :] = jnp.where(low, even, odd)
        if m == 0:
            greet(near)
    for block in range(NZ):
        qs[block * 4 : block * 4 + 4] = (
            s32[block * 64 : (block + 1) * 64, :].astype(BF16).reshape(4, 16, 128)
        )
    lab_in.wait()
    lane = lax.broadcasted_iota(jnp.int32, (1, 128), 1)
    label_row = jnp.zeros((1, 128), jnp.int32)
    for m in range(4):
        label_row = jnp.where(lane % 4 == m, lab_v[0:1, m : m + 1], label_row)
    ls[...] = label_row

    pl.semaphore_wait(barrier, len(far) + len(near))

    for i in range(1, NZ):
        remote(ls, lr.at[i], lab_sem.at[0], lab_sem.at[1], (ahead(i), param)).start()
    for i in range(NZ):
        for s in range(4):
            if i or s:
                remote(
                    qs.at[ahead(i, s)], rb.at[i * 4 + s], zg_send, zg_recv.at[i // PER], (ahead(i, s), param)
                ).start()
    lr[0] = label_row
    home = pltpu.make_async_copy(qs.at[dp], rb.at[0], loc_sem)
    home.start()
    home.wait()
    proj_in.wait()

    def arrange(c):
        first = max(1, c * PER * 4)
        wait_all(rb.at[pl.ds(first, (c + 1) * PER * 4 - first)], zg_recv.at[c])
        for s in range(4):
            for k in range(PER):
                at = (s * PER + k) * 16
                f32s[c, at : at + 16, :] = rb[(c * PER + k) * 4 + s].astype(F32)
        rows = jnp.concatenate(
            [f32s[c, pl.ds(j, 4 * RW, stride=4), :].astype(BF16) for j in range(4)], axis=1
        )
        xs[c] = rows

    def projected(rows, n):
        columns = pl.ds(pl.multiple_of(flip(param, n) * 512, 512), 512)
        return jnp.dot(rows, proj_v[:, columns], preferred_element_type=F32)

    def project(c):
        rows = xs[c]
        for n in range(8):
            part = projected(rows, n)
            for h in range(2):
                own[c, h * 8 + n] = part[2 * h * RW : (2 * h + 1) * RW]
                cs[c, h * 8 + n] = part[(2 * h + 1) * RW : (2 * h + 2) * RW].astype(BF16)
        remote(
            cs.at[c], cr.at[c], core_sem.at[0, c], core_sem.at[1, c], (flip(dp, 1), param)
        ).start()

    def after_core(c):
        wait_all(cr.at[c], core_sem.at[1, c])
        for n in range(16):
            total = own[c, n] + cr[c, n].astype(F32)
            if n:
                sx[c, n] = total.astype(BF16)
                remote(
                    sx.at[c, n], rx.at[c, n], xy_sem.at[0, c], xy_sem.at[1, c], plane_peer(n)
                ).start()
            else:
                own[c, 0] = total

    def after_plane(c):
        wait_all(rx.at[c, pl.ds(1, 15)], xy_sem.at[1, c])
        for j in range(4):
            columns = slice(j * 128, (j + 1) * 128)
            total = own[c, 0, :, columns]
            for n in range(1, 16):
                total += rx[c, n, :, columns].astype(F32)
            dsum[j, c * RW : (c + 1) * RW, :] = total

    def send_examples(c):
        base = c * PER * 16
        for j in range(4):
            for m in range(4):
                zs32[pl.ds(base + j * 4 + m, PER, stride=16), :] = dsum[
                    j, pl.ds(c * RW + m, PER, stride=4), :
                ]
        for k in range(PER):
            i = c * PER + k
            zs[i] = zs32[i * 16 : (i + 1) * 16, :].astype(BF16)
        for i in range(max(1, c * PER), (c + 1) * PER):
            remote(zs.at[i], zr.at[i], zs_sem.at[0], zs_sem.at[1], (behind(i), param)).start()

    for c in range(GROUPS - 1):
        arrange(c)
        project(c)
        if c:
            after_core(c - 1)

    wait_all(lr.at[pl.ds(1, NZ - 1)], lab_sem.at[1])
    labels = jnp.full((1, 128), -1, jnp.int32)
    for i in range(NZ):
        labels = jnp.where(lane // 4 == i, lr[i], labels)
    lq[...] = labels
    for s in (1, 2, 3):
        remote(lq, lqr.at[s - 1], lq_sem.at[0], lq_sem.at[1], (flip(dp, s), param)).start()
    if GROUPS > 1:
        after_core(GROUPS - 2)
    wait_all(lqr, lq_sem.at[1])

    arrange(GROUPS - 1)
    row = lax.broadcasted_iota(jnp.int32, (NT, 4 * NZ), 0)
    tag = row % 8
    for s in range(4):
        tag = jnp.where(row // 8 == s, row % 8 + 8 * flip(q, s), tag)
    sums = jnp.zeros((NT, 512), F32)
    for s in range(4):
        known = labels if s == 0 else lqr[s - 1]
        onehot = (tag == known[:, : 4 * NZ]).astype(BF16)
        rows = jnp.concatenate([xs[c, s * RW : (s + 1) * RW, :] for c in range(GROUPS)], axis=0)
        sums += jnp.dot(onehot, rows, preferred_element_type=F32)
    high = sums.astype(BF16)
    parts = jnp.concatenate([high, (sums - high.astype(F32)).astype(BF16)], axis=0)
    for n in range(8):
        part = projected(parts, n)
        part = part[:NT] + part[NT:]
        for h in range(2):
            town[h * 8 + n] = part[16 * h : 16 * h + 8]
            tcs[h * 8 + n] = part[16 * h + 8 : 16 * h + 16]
    remote(tcs, tcr, tc_sem.at[0], tc_sem.at[1], (flip(dp, 1), param)).start()
    project(GROUPS - 1)

    def stacked(value):
        return jnp.concatenate([value[:, :256], value[:, 256:]], axis=0)

    wait_all(tcr, tc_sem.at[1])
    for n in range(1, 16):
        tsx[n] = stacked(town[n] + tcr[n]).astype(BF16)
        remote(tsx.at[n], trx.at[n], ty_sem.at[0], ty_sem.at[1], plane_peer(n)).start()
    label_sums = stacked(town[0] + tcr[0])
    after_core(GROUPS - 1)
    for c in range(GROUPS - 1):
        after_plane(c)
        send_examples(c)

    wait_all(trx.at[pl.ds(1, 15)], ty_sem.at[1])
    for n in range(1, 16):
        label_sums += trx[n].astype(F32)
    ztb[...] = label_sums.astype(BF16)
    for i in reversed(range(1, NZ)):
        remote(ztb, ztr.at[i], zt_sem.at[0], zt_sem.at[1], (ahead(i), param)).start()
    after_plane(GROUPS - 1)
    send_examples(GROUPS - 1)
    wait_all(ztr.at[pl.ds(1, NZ - 1)], zt_sem.at[1])
    for i in range(1, NZ):
        label_sums += ztr[i].astype(F32)
    agr[q] = jnp.concatenate([label_sums[:8], label_sums[8:]], axis=1)
    for s in (2, 3, 1):
        remote(agr.at[q], agr.at[q], ag_sem.at[0], ag_sem.at[1], (flip(dp, s), param)).start()

    wait_all(zr.at[pl.ds(1, NZ - 1)], zs_sem.at[1])
    mine16 = zs32[0:16, :]
    for i in range(1, NZ):
        mine16 += zr[i].astype(F32)
    mine = jnp.concatenate([mine16[j * 4 : (j + 1) * 4, :] for j in range(4)], axis=1)
    mine = jnp.concatenate([mine, jnp.zeros((4, 512), F32)], axis=0)
    grad_sq = jnp.sum(mine * mine, axis=1, keepdims=True)
    task = lax.broadcasted_iota(jnp.int32, (NT, 128), 0)
    counts = (task == labels).astype(F32)
    for s in range(3):
        counts += (task == lqr[s]).astype(F32)
    counts = jnp.maximum(jnp.sum(counts, axis=1, keepdims=True), 1.0)

    wait_all(agr.at[pl.ds(0, 3)], ag_sem.at[1])
    means = agr[...].reshape(NT, 512) / counts
    means_ref[...] = means
    contract = (((1,), (1,)), ((), ()))
    dots = lax.dot_general(mine, means, contract, precision=HIGHEST, preferred_element_type=F32)
    mean_sq = lax.dot_general(
        jnp.ones((8, 512), F32), means * means, contract, precision=HIGHEST, preferred_element_type=F32
    )
    pks[:, 0:64] = jnp.concatenate([dots, mean_sq], axis=1)
    pks[:, 64:128] = jnp.broadcast_to(grad_sq, (8, 64))
    for n in range(1, 8):
        remote(pks, pkr.at[n - 1], pk_sem.at[0], pk_sem.at[1], (dp, flip(param, n))).start()
    wait_all(rb.at[pl.ds(1, 4 * NZ - 1)], zg_send)
    wait_all(lr.at[pl.ds(1, NZ - 1)], lab_sem.at[0])
    wait_all(lqr, lq_sem.at[0])
    for c in range(GROUPS):
        wait_all(cs.at[c], core_sem.at[0, c])
        wait_all(sx.at[c, pl.ds(1, 15)], xy_sem.at[0, c])
    wait_all(zs.at[pl.ds(1, NZ - 1)], zs_sem.at[0])
    wait_all(tcs, tc_sem.at[0])
    wait_all(tsx.at[pl.ds(1, 15)], ty_sem.at[0])
    wait_all(ztr.at[pl.ds(1, NZ - 1)], zt_sem.at[0])
    wait_all(agr.at[pl.ds(0, 3)], ag_sem.at[0])
    wait_all(pkr, pk_sem.at[1])
    total = pks[...]
    for n in range(7):
        total += pkr[n]
    scores_ref[...] = (
        total[0:4, 0:NT]
        / K
        * lax.rsqrt(total[0:4, 64 : 64 + NT] / K + EPSILON)
        * lax.rsqrt(total[0:4, NT : 2 * NT] / K + EPSILON)
    )
    wait_all(pkr, pk_sem.at[0])


def body(output_gradient, adapter_activations, proj, labels):
    proj = proj.reshape(proj.shape[0] * proj.shape[1], proj.shape[2])
    vm = pltpu.VMEM
    scratch = [
        vm((1024, 512), BF16),
        vm((64, 1024), BF16),
        vm((512, K), BF16),
        vm((1, 4), jnp.int32),
        vm((4, 512, 128), F32),
        vm((1024, 128), F32),
        vm((4 * NZ, 16, 128), BF16),
        vm((4 * NZ, 16, 128), BF16),
        vm((GROUPS, PER * 64, 128), F32),
        vm((1, 128), jnp.int32),
        vm((NZ, 1, 128), jnp.int32),
        vm((1, 128), jnp.int32),
        vm((3, 1, 128), jnp.int32),
        vm((GROUPS, 4 * RW, 512), BF16),
        vm((GROUPS, 16, RW, 512), F32),
        vm((GROUPS, 16, RW, 512), BF16),
        vm((GROUPS, 16, RW, 512), BF16),
        vm((GROUPS, 16, RW, 512), BF16),
        vm((GROUPS, 16, RW, 512), BF16),
        vm((4, 4 * NZ, 128), F32),
        vm((16 * NZ, 128), F32),
        vm((NZ, 16, 128), BF16),
        vm((NZ, 16, 128), BF16),
        vm((16, 8, 512), F32),
        vm((16, 8, 512), F32),
        vm((16, 8, 512), F32),
        vm((16, 16, 256), BF16),
        vm((16, 16, 256), BF16),
        vm((16, 256), BF16),
        vm((NZ, 16, 256), BF16),
        vm((4, 8, 512), F32),
        vm((8, 128), F32),
        vm((7, 8, 128), F32),
    ]
    dma = pltpu.SemaphoreType.DMA
    scratch += [
        dma((7,)),
        dma(()),
        dma((2,)),
        dma((2,)),
        dma(()),
        dma((GROUPS,)),
        dma((2, GROUPS)),
        dma((2, GROUPS)),
        dma((2,)),
        dma((2,)),
        dma((2,)),
        dma((2,)),
        dma((2,)),
        dma((2,)),
    ]
    hbm = pl.BlockSpec(memory_space=pl.ANY)
    vmem = pl.BlockSpec(memory_space=pltpu.VMEM)
    return pl.pallas_call(
        kernel,
        out_shape=(
            jax.ShapeDtypeStruct((4, NT), F32),
            jax.ShapeDtypeStruct((NT, 512), F32),
        ),
        in_specs=[hbm, hbm, hbm, hbm],
        out_specs=(vmem, vmem),
        scratch_shapes=scratch,
        compiler_params=pltpu.CompilerParams(
            collective_id=0, has_side_effects=True, vmem_limit_bytes=55040 * 1024
        ),
    )(output_gradient, adapter_activations.T, proj, labels.reshape(1, 4))


def solution(mesh):
    placed = (P("dp", "param"), P("dp", None), P(("param", "dp"), None, None), P("dp"))
    return jax.shard_map(
        body,
        mesh=mesh,
        in_specs=placed,
        out_specs=(P("dp", None), P(None, "param")),
        check_vma=False,
    )
```

```python
import jax
import jax.numpy as jnp
from jax import lax
from jax.experimental import pallas as pl
from jax.experimental.pallas import tpu as pltpu
from jax.sharding import PartitionSpec as P

K = 4096
NT = 32
EPSILON = 1e-06
MESH = pl.DeviceIdType.MESH
F32 = jnp.float32
BF16 = jnp.bfloat16
HIGHEST = lax.Precision.HIGHEST

OFFSETS = (0, 1, 15, 2, 14, 3, 13, 4, 12, 5, 11, 6, 10, 7, 9, 8)
NZ = 16
GROUPS = 2
PER = NZ // GROUPS
RW = PER * 4


def flip(value, bits):
    for bit in (1, 2, 4):
        if bits & bit:
            value = value + bit - 2 * bit * ((value // bit) % 2)
    return value


def kernel(
    og_h, act_h, proj_h, lab_h, scores_ref, means_ref,
    og_v, act_v, proj_v, lab_v, g32, s32, qs, rb, f32s, ls, lr, lq, lqr,
    xs, own, cs, cr, sx, rx, dsum, zs32, zs, zr,
    town, tcs, tcr, tsx, trx, ztb, ztr, agr, pks, pkr,
    in_sem, loc_sem, lab_sem, lq_sem, zg_send, zg_recv, core_sem, xy_sem,
    zs_sem, tc_sem, ty_sem, zt_sem, ag_sem, pk_sem,
):
    dp, param = lax.axis_index("dp"), lax.axis_index("param")
    z, q = dp // 4, dp % 4
    xl, y = param // 4, param % 4

    def ahead(i, s=0):
        return ((z + OFFSETS[i]) % NZ) * 4 + flip(q, s)

    def behind(i, s=0):
        return ((z + NZ - OFFSETS[i]) % NZ) * 4 + flip(q, s)

    def plane_peer(n):
        return (flip(dp, (n // 8) * 2), flip(param, n % 8))

    def remote(src, dst, send, recv, device):
        return pltpu.make_async_remote_copy(
            src_ref=src, dst_ref=dst, send_sem=send, recv_sem=recv,
            device_id=device, device_id_type=MESH,
        )

    def wait_all(ref, sem):
        pltpu.make_async_copy(ref, ref, sem).wait()

    act_in = pltpu.make_async_copy(act_h, act_v, in_sem.at[0])
    act_in.start()
    lab_in = pltpu.make_async_copy(lab_h, lab_v, in_sem.at[6])
    lab_in.start()
    og_in = []
    for m in range(4):
        copy = pltpu.make_async_copy(
            og_h.at[pl.ds(m * 256, 256)], og_v.at[pl.ds(m * 256, 256)], in_sem.at[2 + m]
        )
        copy.start()
        og_in.append(copy)
    proj_in = pltpu.make_async_copy(proj_h, proj_v, in_sem.at[1])
    proj_in.start()

    barrier = pltpu.get_barrier_semaphore()
    far = [(ahead(i, s), param) for i in reversed(range(9, NZ)) for s in range(4)]
    near = [(ahead(i, s), param) for i in reversed(range(9)) for s in range(4) if i or s]
    near += [plane_peer(n) for n in range(1, 16) if n != 8]

    def greet(peers):
        for peer in peers:
            pl.semaphore_signal(barrier, inc=1, device_id=peer, device_id_type=MESH)

    greet(far)

    act_in.wait()
    low = lax.broadcasted_iota(jnp.int32, (64, 128), 1) < 64
    for m in range(4):
        og_in[m].wait()
        act = act_v[:, m * 256 : (m + 1) * 256]
        g32[m] = lax.dot_general(
            og_v[m * 256 : (m + 1) * 256, :],
            jnp.concatenate([act, act], axis=0),
            (((0,), (1,)), ((), ())),
            preferred_element_type=F32,
        )
        for j in range(4):
            even = g32[m, pl.ds(2 * j, 64, stride=8), :]
            odd = g32[m, pl.ds(2 * j + 1, 64, stride=8), :]
            s32[pl.ds(m * 4 + j, 64, stride=16), :] = jnp.where(low, even, odd)
        if m == 0:
            greet(near)
    for block in range(NZ):
        qs[block * 4 : block * 4 + 4] = (
            s32[block * 64 : (block + 1) * 64, :].astype(BF16).reshape(4, 16, 128)
        )
    lab_in.wait()
    lane = lax.broadcasted_iota(jnp.int32, (1, 128), 1)
    label_row = jnp.zeros((1, 128), jnp.int32)
    for m in range(4):
        label_row = jnp.where(lane % 4 == m, lab_v[0:1, m : m + 1], label_row)
    ls[...] = label_row

    pl.semaphore_wait(barrier, len(far) + len(near))

    for i in range(1, NZ):
        remote(ls, lr.at[i], lab_sem.at[0], lab_sem.at[1], (ahead(i), param)).start()
    for i in range(NZ):
        for s in range(4):
            if i or s:
                remote(
                    qs.at[ahead(i, s)], rb.at[i * 4 + s], zg_send, zg_recv.at[i // PER], (ahead(i, s), param)
                ).start()
    lr[0] = label_row
    home = pltpu.make_async_copy(qs.at[dp], rb.at[0], loc_sem)
    home.start()
    home.wait()
    proj_in.wait()

    def arrange(c):
        first = max(1, c * PER * 4)
        wait_all(rb.at[pl.ds(first, (c + 1) * PER * 4 - first)], zg_recv.at[c])
        for s in range(4):
            for k in range(PER):
                at = (s * PER + k) * 16
                f32s[c, at : at + 16, :] = rb[(c * PER + k) * 4 + s].astype(F32)
        rows = jnp.concatenate(
            [f32s[c, pl.ds(j, 4 * RW, stride=4), :].astype(BF16) for j in range(4)], axis=1
        )
        xs[c] = rows

    def projected(rows, n):
        columns = pl.ds(pl.multiple_of(flip(param, n) * 512, 512), 512)
        return jnp.dot(rows, proj_v[:, columns], preferred_element_type=F32)

    def project(c):
        rows = xs[c]
        for n in range(8):
            part = projected(rows, n)
            for h in range(2):
                own[c, h * 8 + n] = part[2 * h * RW : (2 * h + 1) * RW]
                cs[c, h * 8 + n] = part[(2 * h + 1) * RW : (2 * h + 2) * RW].astype(BF16)
        remote(
            cs.at[c], cr.at[c], core_sem.at[0, c], core_sem.at[1, c], (flip(dp, 1), param)
        ).start()

    def after_core(c):
        wait_all(cr.at[c], core_sem.at[1, c])
        for n in range(16):
            total = own[c, n] + cr[c, n].astype(F32)
            if n:
                sx[c, n] = total.astype(BF16)
                remote(
                    sx.at[c, n], rx.at[c, n], xy_sem.at[0, c], xy_sem.at[1, c], plane_peer(n)
                ).start()
            else:
                own[c, 0] = total

    def after_plane(c):
        wait_all(rx.at[c, pl.ds(1, 15)], xy_sem.at[1, c])
        for j in range(4):
            columns = slice(j * 128, (j + 1) * 128)
            total = own[c, 0, :, columns]
            for n in range(1, 16):
                total += rx[c, n, :, columns].astype(F32)
            dsum[j, c * RW : (c + 1) * RW, :] = total

    def send_examples(c):
        base = c * PER * 16
        for j in range(4):
            for m in range(4):
                zs32[pl.ds(base + j * 4 + m, PER, stride=16), :] = dsum[
                    j, pl.ds(c * RW + m, PER, stride=4), :
                ]
        for k in range(PER):
            i = c * PER + k
            zs[i] = zs32[i * 16 : (i + 1) * 16, :].astype(BF16)
        for i in range(max(1, c * PER), (c + 1) * PER):
            remote(zs.at[i], zr.at[i], zs_sem.at[0], zs_sem.at[1], (behind(i), param)).start()

    for c in range(GROUPS - 1):
        arrange(c)
        project(c)
        if c:
            after_core(c - 1)

    wait_all(lr.at[pl.ds(1, NZ - 1)], lab_sem.at[1])
    labels = jnp.full((1, 128), -1, jnp.int32)
    for i in range(NZ):
        labels = jnp.where(lane // 4 == i, lr[i], labels)
    lq[...] = labels
    for s in (1, 2, 3):
        remote(lq, lqr.at[s - 1], lq_sem.at[0], lq_sem.at[1], (flip(dp, s), param)).start()
    if GROUPS > 1:
        after_core(GROUPS - 2)
    wait_all(lqr, lq_sem.at[1])

    arrange(GROUPS - 1)
    row = lax.broadcasted_iota(jnp.int32, (NT, 4 * NZ), 0)
    tag = row % 8
    for s in range(4):
        tag = jnp.where(row // 8 == s, row % 8 + 8 * flip(q, s), tag)
    sums = jnp.zeros((NT, 512), F32)
    for s in range(4):
        known = labels if s == 0 else lqr[s - 1]
        onehot = (tag == known[:, : 4 * NZ]).astype(BF16)
        rows = jnp.concatenate([xs[c, s * RW : (s + 1) * RW, :] for c in range(GROUPS)], axis=0)
        sums += jnp.dot(onehot, rows, preferred_element_type=F32)
    high = sums.astype(BF16)
    parts = jnp.concatenate([high, (sums - high.astype(F32)).astype(BF16)], axis=0)
    for n in range(8):
        part = projected(parts, n)
        part = part[:NT] + part[NT:]
        for h in range(2):
            town[h * 8 + n] = part[16 * h : 16 * h + 8]
            tcs[h * 8 + n] = part[16 * h + 8 : 16 * h + 16]
    remote(tcs, tcr, tc_sem.at[0], tc_sem.at[1], (flip(dp, 1), param)).start()
    project(GROUPS - 1)

    def stacked(value):
        return jnp.concatenate([value[:, :256], value[:, 256:]], axis=0)

    wait_all(tcr, tc_sem.at[1])
    for n in range(1, 16):
        tsx[n] = stacked(town[n] + tcr[n]).astype(BF16)
        remote(tsx.at[n], trx.at[n], ty_sem.at[0], ty_sem.at[1], plane_peer(n)).start()
    label_sums = stacked(town[0] + tcr[0])
    after_core(GROUPS - 1)
    for c in range(GROUPS - 1):
        after_plane(c)
        send_examples(c)

    wait_all(trx.at[pl.ds(1, 15)], ty_sem.at[1])
    for n in range(1, 16):
        label_sums += trx[n].astype(F32)
    ztb[...] = label_sums.astype(BF16)
    for i in reversed(range(1, NZ)):
        remote(ztb, ztr.at[i], zt_sem.at[0], zt_sem.at[1], (ahead(i), param)).start()
    after_plane(GROUPS - 1)
    send_examples(GROUPS - 1)
    wait_all(ztr.at[pl.ds(1, NZ - 1)], zt_sem.at[1])
    for i in range(1, NZ):
        label_sums += ztr[i].astype(F32)
    agr[q] = jnp.concatenate([label_sums[:8], label_sums[8:]], axis=1)
    for s in (2, 3, 1):
        remote(agr.at[q], agr.at[q], ag_sem.at[0], ag_sem.at[1], (flip(dp, s), param)).start()

    wait_all(zr.at[pl.ds(1, NZ - 1)], zs_sem.at[1])
    mine16 = zs32[0:16, :]
    for i in range(1, NZ):
        mine16 += zr[i].astype(F32)
    mine = jnp.concatenate([mine16[j * 4 : (j + 1) * 4, :] for j in range(4)], axis=1)
    mine = jnp.concatenate([mine, jnp.zeros((4, 512), F32)], axis=0)
    grad_sq = jnp.sum(mine * mine, axis=1, keepdims=True)
    task = lax.broadcasted_iota(jnp.int32, (NT, 128), 0)
    counts = (task == labels).astype(F32)
    for s in range(3):
        counts += (task == lqr[s]).astype(F32)
    counts = jnp.maximum(jnp.sum(counts, axis=1, keepdims=True), 1.0)

    wait_all(agr.at[pl.ds(0, 3)], ag_sem.at[1])
    means = agr[...].reshape(NT, 512) / counts
    means_ref[...] = means
    contract = (((1,), (1,)), ((), ()))
    dots = lax.dot_general(mine, means, contract, precision=HIGHEST, preferred_element_type=F32)
    mean_sq = lax.dot_general(
        jnp.ones((8, 512), F32), means * means, contract, precision=HIGHEST, preferred_element_type=F32
    )
    pks[:, 0:64] = jnp.concatenate([dots, mean_sq], axis=1)
    pks[:, 64:128] = jnp.broadcast_to(grad_sq, (8, 64))
    for n in range(1, 8):
        remote(pks, pkr.at[n - 1], pk_sem.at[0], pk_sem.at[1], (dp, flip(param, n))).start()
    wait_all(rb.at[pl.ds(1, 4 * NZ - 1)], zg_send)
    wait_all(lr.at[pl.ds(1, NZ - 1)], lab_sem.at[0])
    wait_all(lqr, lq_sem.at[0])
    for c in range(GROUPS):
        wait_all(cs.at[c], core_sem.at[0, c])
        wait_all(sx.at[c, pl.ds(1, 15)], xy_sem.at[0, c])
    wait_all(zs.at[pl.ds(1, NZ - 1)], zs_sem.at[0])
    wait_all(tcs, tc_sem.at[0])
    wait_all(tsx.at[pl.ds(1, 15)], ty_sem.at[0])
    wait_all(ztr.at[pl.ds(1, NZ - 1)], zt_sem.at[0])
    wait_all(agr.at[pl.ds(0, 3)], ag_sem.at[0])
    wait_all(pkr, pk_sem.at[1])
    total = pks[...]
    for n in range(7):
        total += pkr[n]
    scores_ref[...] = (
        total[0:4, 0:NT]
        / K
        * lax.rsqrt(total[0:4, 64 : 64 + NT] / K + EPSILON)
        * lax.rsqrt(total[0:4, NT : 2 * NT] / K + EPSILON)
    )
    wait_all(pkr, pk_sem.at[0])


def body(output_gradient, adapter_activations, proj, labels):
    proj = proj.reshape(proj.shape[0] * proj.shape[1], proj.shape[2])
    vm = pltpu.VMEM
    scratch = [
        vm((1024, 512), BF16),
        vm((64, 1024), BF16),
        vm((512, K), BF16),
        vm((1, 4), jnp.int32),
        vm((4, 512, 128), F32),
        vm((1024, 128), F32),
        vm((4 * NZ, 16, 128), BF16),
        vm((4 * NZ, 16, 128), BF16),
        vm((GROUPS, PER * 64, 128), F32),
        vm((1, 128), jnp.int32),
        vm((NZ, 1, 128), jnp.int32),
        vm((1, 128), jnp.int32),
        vm((3, 1, 128), jnp.int32),
        vm((GROUPS, 4 * RW, 512), BF16),
        vm((GROUPS, 16, RW, 512), F32),
        vm((GROUPS, 16, RW, 512), BF16),
        vm((GROUPS, 16, RW, 512), BF16),
        vm((GROUPS, 16, RW, 512), BF16),
        vm((GROUPS, 16, RW, 512), BF16),
        vm((4, 4 * NZ, 128), F32),
        vm((16 * NZ, 128), F32),
        vm((NZ, 16, 128), BF16),
        vm((NZ, 16, 128), BF16),
        vm((16, 8, 512), F32),
        vm((16, 8, 512), F32),
        vm((16, 8, 512), F32),
        vm((16, 16, 256), BF16),
        vm((16, 16, 256), BF16),
        vm((16, 256), BF16),
        vm((NZ, 16, 256), BF16),
        vm((4, 8, 512), F32),
        vm((8, 128), F32),
        vm((7, 8, 128), F32),
    ]
    dma = pltpu.SemaphoreType.DMA
    scratch += [
        dma((7,)),
        dma(()),
        dma((2,)),
        dma((2,)),
        dma(()),
        dma((GROUPS,)),
        dma((2, GROUPS)),
        dma((2, GROUPS)),
        dma((2,)),
        dma((2,)),
        dma((2,)),
        dma((2,)),
        dma((2,)),
        dma((2,)),
    ]
    hbm = pl.BlockSpec(memory_space=pl.ANY)
    vmem = pl.BlockSpec(memory_space=pltpu.VMEM)
    return pl.pallas_call(
        kernel,
        out_shape=(
            jax.ShapeDtypeStruct((4, NT), F32),
            jax.ShapeDtypeStruct((NT, 512), F32),
        ),
        in_specs=[hbm, hbm, hbm, hbm],
        out_specs=(vmem, vmem),
        scratch_shapes=scratch,
        compiler_params=pltpu.CompilerParams(
            collective_id=0, has_side_effects=True, vmem_limit_bytes=55040 * 1024
        ),
    )(output_gradient, adapter_activations.T, proj, labels.reshape(1, 4))


def solution(mesh):
    placed = (P("dp", "param"), P("dp", None), P(("param", "dp"), None, None), P("dp"))
    return jax.shard_map(
        body,
        mesh=mesh,
        in_specs=placed,
        out_specs=(P("dp", None), P(None, "param")),
        check_vma=False,
    )
```

```python
import jax
import jax.numpy as jnp
from jax import lax
from jax.experimental import pallas as pl
from jax.experimental.pallas import tpu as pltpu
from jax.sharding import PartitionSpec as P

K = 4096
NT = 32
EPSILON = 1e-06
MESH = pl.DeviceIdType.MESH
F32 = jnp.float32
BF16 = jnp.bfloat16
HIGHEST = lax.Precision.HIGHEST

OFFSETS = (0, 1, 15, 2, 14, 3, 13, 4, 12, 5, 11, 6, 10, 7, 9, 8)
NZ = 16
GROUPS = 2
PER = NZ // GROUPS
RW = PER * 4


def flip(value, bits):
    for bit in (1, 2, 4):
        if bits & bit:
            value = value + bit - 2 * bit * ((value // bit) % 2)
    return value


def kernel(
    og_h, act_h, proj_h, lab_h, scores_ref, means_ref,
    og_v, act_v, proj_v, lab_v, g32, s32, qs, rb, f32s, ls, lr, lq, lqr,
    xs, own, cs, cr, sx, rx, dsum, zs32, zs, zr,
    town, tcs, tcr, tsx, trx, ztb, ztr, agr, pks, pkr,
    in_sem, loc_sem, lab_sem, lq_sem, zg_send, zg_recv, core_sem, xy_sem,
    zs_sem, tc_sem, ty_sem, zt_sem, ag_sem, pk_sem,
):
    dp, param = lax.axis_index("dp"), lax.axis_index("param")
    z, q = dp // 4, dp % 4
    xl, y = param // 4, param % 4

    def ahead(i, s=0):
        return ((z + OFFSETS[i]) % NZ) * 4 + flip(q, s)

    def behind(i, s=0):
        return ((z + NZ - OFFSETS[i]) % NZ) * 4 + flip(q, s)

    def plane_peer(n):
        return (flip(dp, (n // 8) * 2), flip(param, n % 8))

    def remote(src, dst, send, recv, device):
        return pltpu.make_async_remote_copy(
            src_ref=src, dst_ref=dst, send_sem=send, recv_sem=recv,
            device_id=device, device_id_type=MESH,
        )

    def wait_all(ref, sem):
        pltpu.make_async_copy(ref, ref, sem).wait()

    act_in = pltpu.make_async_copy(act_h, act_v, in_sem.at[0])
    act_in.start()
    lab_in = pltpu.make_async_copy(lab_h, lab_v, in_sem.at[6])
    lab_in.start()
    og_in = []
    for m in range(4):
        copy = pltpu.make_async_copy(
            og_h.at[pl.ds(m * 256, 256)], og_v.at[pl.ds(m * 256, 256)], in_sem.at[2 + m]
        )
        copy.start()
        og_in.append(copy)
    proj_in = pltpu.make_async_copy(proj_h, proj_v, in_sem.at[1])
    proj_in.start()

    barrier = pltpu.get_barrier_semaphore()
    far = [(ahead(i, s), param) for i in reversed(range(9, NZ)) for s in range(4)]
    near = [(ahead(i, s), param) for i in reversed(range(9)) for s in range(4) if i or s]
    near += [plane_peer(n) for n in range(1, 16) if n != 8]

    def greet(peers):
        for peer in peers:
            pl.semaphore_signal(barrier, inc=1, device_id=peer, device_id_type=MESH)

    greet(far)

    act_in.wait()
    low = lax.broadcasted_iota(jnp.int32, (64, 128), 1) < 64
    for m in range(4):
        og_in[m].wait()
        act = act_v[:, m * 256 : (m + 1) * 256]
        g32[m] = lax.dot_general(
            og_v[m * 256 : (m + 1) * 256, :],
            jnp.concatenate([act, act], axis=0),
            (((0,), (1,)), ((), ())),
            preferred_element_type=F32,
        )
        for j in range(4):
            even = g32[m, pl.ds(2 * j, 64, stride=8), :]
            odd = g32[m, pl.ds(2 * j + 1, 64, stride=8), :]
            s32[pl.ds(m * 4 + j, 64, stride=16), :] = jnp.where(low, even, odd)
        if m == 0:
            greet(near)
    for block in range(NZ):
        qs[block * 4 : block * 4 + 4] = (
            s32[block * 64 : (block + 1) * 64, :].astype(BF16).reshape(4, 16, 128)
        )
    lab_in.wait()
    lane = lax.broadcasted_iota(jnp.int32, (1, 128), 1)
    label_row = jnp.zeros((1, 128), jnp.int32)
    for m in range(4):
        label_row = jnp.where(lane % 4 == m, lab_v[0:1, m : m + 1], label_row)
    ls[...] = label_row

    pl.semaphore_wait(barrier, len(far) + len(near))

    for i in range(1, NZ):
        remote(ls, lr.at[i], lab_sem.at[0], lab_sem.at[1], (ahead(i), param)).start()
    for i in range(NZ):
        for s in range(4):
            if i or s:
                remote(
                    qs.at[ahead(i, s)], rb.at[i * 4 + s], zg_send, zg_recv.at[i // PER], (ahead(i, s), param)
                ).start()
    lr[0] = label_row
    home = pltpu.make_async_copy(qs.at[dp], rb.at[0], loc_sem)
    home.start()
    home.wait()
    proj_in.wait()

    def arrange(c):
        first = max(1, c * PER * 4)
        wait_all(rb.at[pl.ds(first, (c + 1) * PER * 4 - first)], zg_recv.at[c])
        for s in range(4):
            for k in range(PER):
                at = (s * PER + k) * 16
                f32s[c, at : at + 16, :] = rb[(c * PER + k) * 4 + s].astype(F32)
        rows = jnp.concatenate(
            [f32s[c, pl.ds(j, 4 * RW, stride=4), :].astype(BF16) for j in range(4)], axis=1
        )
        xs[c] = rows

    def projected(rows, n):
        columns = pl.ds(pl.multiple_of(flip(param, n) * 512, 512), 512)
        return jnp.dot(rows, proj_v[:, columns], preferred_element_type=F32)

    def project(c):
        rows = xs[c]
        for n in range(8):
            part = projected(rows, n)
            for h in range(2):
                own[c, h * 8 + n] = part[2 * h * RW : (2 * h + 1) * RW]
                cs[c, h * 8 + n] = part[(2 * h + 1) * RW : (2 * h + 2) * RW].astype(BF16)
        remote(
            cs.at[c], cr.at[c], core_sem.at[0, c], core_sem.at[1, c], (flip(dp, 1), param)
        ).start()

    def after_core(c):
        wait_all(cr.at[c], core_sem.at[1, c])
        for n in range(16):
            total = own[c, n] + cr[c, n].astype(F32)
            if n:
                sx[c, n] = total.astype(BF16)
                remote(
                    sx.at[c, n], rx.at[c, n], xy_sem.at[0, c], xy_sem.at[1, c], plane_peer(n)
                ).start()
            else:
                own[c, 0] = total

    def after_plane(c):
        wait_all(rx.at[c, pl.ds(1, 15)], xy_sem.at[1, c])
        for j in range(4):
            columns = slice(j * 128, (j + 1) * 128)
            total = own[c, 0, :, columns]
            for n in range(1, 16):
                total += rx[c, n, :, columns].astype(F32)
            dsum[j, c * RW : (c + 1) * RW, :] = total

    def send_examples(c):
        base = c * PER * 16
        for j in range(4):
            for m in range(4):
                zs32[pl.ds(base + j * 4 + m, PER, stride=16), :] = dsum[
                    j, pl.ds(c * RW + m, PER, stride=4), :
                ]
        for k in range(PER):
            i = c * PER + k
            zs[i] = zs32[i * 16 : (i + 1) * 16, :].astype(BF16)
        for i in range(max(1, c * PER), (c + 1) * PER):
            remote(zs.at[i], zr.at[i], zs_sem.at[0], zs_sem.at[1], (behind(i), param)).start()

    for c in range(GROUPS - 1):
        arrange(c)
        project(c)
        if c:
            after_core(c - 1)

    wait_all(lr.at[pl.ds(1, NZ - 1)], lab_sem.at[1])
    labels = jnp.full((1, 128), -1, jnp.int32)
    for i in range(NZ):
        labels = jnp.where(lane // 4 == i, lr[i], labels)
    lq[...] = labels
    for s in (1, 2, 3):
        remote(lq, lqr.at[s - 1], lq_sem.at[0], lq_sem.at[1], (flip(dp, s), param)).start()
    if GROUPS > 1:
        after_core(GROUPS - 2)
    wait_all(lqr, lq_sem.at[1])

    arrange(GROUPS - 1)
    row = lax.broadcasted_iota(jnp.int32, (NT, 4 * NZ), 0)
    tag = row % 8
    for s in range(4):
        tag = jnp.where(row // 8 == s, row % 8 + 8 * flip(q, s), tag)
    sums = jnp.zeros((NT, 512), F32)
    for s in range(4):
        known = labels if s == 0 else lqr[s - 1]
        onehot = (tag == known[:, : 4 * NZ]).astype(BF16)
        rows = jnp.concatenate([xs[c, s * RW : (s + 1) * RW, :] for c in range(GROUPS)], axis=0)
        sums += jnp.dot(onehot, rows, preferred_element_type=F32)
    high = sums.astype(BF16)
    parts = jnp.concatenate([high, (sums - high.astype(F32)).astype(BF16)], axis=0)
    for n in range(8):
        part = projected(parts, n)
        part = part[:NT] + part[NT:]
        for h in range(2):
            town[h * 8 + n] = part[16 * h : 16 * h + 8]
            tcs[h * 8 + n] = part[16 * h + 8 : 16 * h + 16]
    remote(tcs, tcr, tc_sem.at[0], tc_sem.at[1], (flip(dp, 1), param)).start()
    project(GROUPS - 1)

    def stacked(value):
        return jnp.concatenate([value[:, :256], value[:, 256:]], axis=0)

    wait_all(tcr, tc_sem.at[1])
    for n in range(1, 16):
        tsx[n] = stacked(town[n] + tcr[n]).astype(BF16)
        remote(tsx.at[n], trx.at[n], ty_sem.at[0], ty_sem.at[1], plane_peer(n)).start()
    label_sums = stacked(town[0] + tcr[0])
    after_core(GROUPS - 1)
    for c in range(GROUPS - 1):
        after_plane(c)
        send_examples(c)

    wait_all(trx.at[pl.ds(1, 15)], ty_sem.at[1])
    for n in range(1, 16):
        label_sums += trx[n].astype(F32)
    ztb[...] = label_sums.astype(BF16)
    for i in reversed(range(1, NZ)):
        remote(ztb, ztr.at[i], zt_sem.at[0], zt_sem.at[1], (ahead(i), param)).start()
    after_plane(GROUPS - 1)
    send_examples(GROUPS - 1)
    wait_all(ztr.at[pl.ds(1, NZ - 1)], zt_sem.at[1])
    for i in range(1, NZ):
        label_sums += ztr[i].astype(F32)
    agr[q] = jnp.concatenate([label_sums[:8], label_sums[8:]], axis=1)
    for s in (2, 3, 1):
        remote(agr.at[q], agr.at[q], ag_sem.at[0], ag_sem.at[1], (flip(dp, s), param)).start()

    wait_all(zr.at[pl.ds(1, NZ - 1)], zs_sem.at[1])
    mine16 = zs32[0:16, :]
    for i in range(1, NZ):
        mine16 += zr[i].astype(F32)
    mine = jnp.concatenate([mine16[j * 4 : (j + 1) * 4, :] for j in range(4)], axis=1)
    mine = jnp.concatenate([mine, jnp.zeros((4, 512), F32)], axis=0)
    grad_sq = jnp.sum(mine * mine, axis=1, keepdims=True)
    task = lax.broadcasted_iota(jnp.int32, (NT, 128), 0)
    counts = (task == labels).astype(F32)
    for s in range(3):
        counts += (task == lqr[s]).astype(F32)
    counts = jnp.maximum(jnp.sum(counts, axis=1, keepdims=True), 1.0)

    wait_all(agr.at[pl.ds(0, 3)], ag_sem.at[1])
    means = agr[...].reshape(NT, 512) / counts
    means_ref[...] = means
    contract = (((1,), (1,)), ((), ()))
    dots = lax.dot_general(mine, means, contract, precision=HIGHEST, preferred_element_type=F32)
    squares = means * means
    high = squares.astype(BF16)
    ones = jnp.ones((8, 512), BF16)
    mean_sq = lax.dot_general(ones, high, contract, preferred_element_type=F32)
    rest = (squares - high.astype(F32)).astype(BF16)
    mean_sq += lax.dot_general(ones, rest, contract, preferred_element_type=F32)
    pks[:, 0:64] = jnp.concatenate([dots, mean_sq], axis=1)
    pks[:, 64:128] = jnp.broadcast_to(grad_sq, (8, 64))
    for n in range(1, 8):
        remote(pks, pkr.at[n - 1], pk_sem.at[0], pk_sem.at[1], (dp, flip(param, n))).start()
    wait_all(rb.at[pl.ds(1, 4 * NZ - 1)], zg_send)
    wait_all(lr.at[pl.ds(1, NZ - 1)], lab_sem.at[0])
    wait_all(lqr, lq_sem.at[0])
    for c in range(GROUPS):
        wait_all(cs.at[c], core_sem.at[0, c])
        wait_all(sx.at[c, pl.ds(1, 15)], xy_sem.at[0, c])
    wait_all(zs.at[pl.ds(1, NZ - 1)], zs_sem.at[0])
    wait_all(tcs, tc_sem.at[0])
    wait_all(tsx.at[pl.ds(1, 15)], ty_sem.at[0])
    wait_all(ztr.at[pl.ds(1, NZ - 1)], zt_sem.at[0])
    wait_all(agr.at[pl.ds(0, 3)], ag_sem.at[0])
    wait_all(pkr, pk_sem.at[1])
    total = pks[...]
    for n in range(7):
        total += pkr[n]
    scores_ref[...] = (
        total[0:4, 0:NT]
        / K
        * lax.rsqrt(total[0:4, 64 : 64 + NT] / K + EPSILON)
        * lax.rsqrt(total[0:4, NT : 2 * NT] / K + EPSILON)
    )
    wait_all(pkr, pk_sem.at[0])


def body(output_gradient, adapter_activations, proj, labels):
    proj = proj.reshape(proj.shape[0] * proj.shape[1], proj.shape[2])
    vm = pltpu.VMEM
    scratch = [
        vm((1024, 512), BF16),
        vm((64, 1024), BF16),
        vm((512, K), BF16),
        vm((1, 4), jnp.int32),
        vm((4, 512, 128), F32),
        vm((1024, 128), F32),
        vm((4 * NZ, 16, 128), BF16),
        vm((4 * NZ, 16, 128), BF16),
        vm((GROUPS, PER * 64, 128), F32),
        vm((1, 128), jnp.int32),
        vm((NZ, 1, 128), jnp.int32),
        vm((1, 128), jnp.int32),
        vm((3, 1, 128), jnp.int32),
        vm((GROUPS, 4 * RW, 512), BF16),
        vm((GROUPS, 16, RW, 512), F32),
        vm((GROUPS, 16, RW, 512), BF16),
        vm((GROUPS, 16, RW, 512), BF16),
        vm((GROUPS, 16, RW, 512), BF16),
        vm((GROUPS, 16, RW, 512), BF16),
        vm((4, 4 * NZ, 128), F32),
        vm((16 * NZ, 128), F32),
        vm((NZ, 16, 128), BF16),
        vm((NZ, 16, 128), BF16),
        vm((16, 8, 512), F32),
        vm((16, 8, 512), F32),
        vm((16, 8, 512), F32),
        vm((16, 16, 256), BF16),
        vm((16, 16, 256), BF16),
        vm((16, 256), BF16),
        vm((NZ, 16, 256), BF16),
        vm((4, 8, 512), F32),
        vm((8, 128), F32),
        vm((7, 8, 128), F32),
    ]
    dma = pltpu.SemaphoreType.DMA
    scratch += [
        dma((7,)),
        dma(()),
        dma((2,)),
        dma((2,)),
        dma(()),
        dma((GROUPS,)),
        dma((2, GROUPS)),
        dma((2, GROUPS)),
        dma((2,)),
        dma((2,)),
        dma((2,)),
        dma((2,)),
        dma((2,)),
        dma((2,)),
    ]
    hbm = pl.BlockSpec(memory_space=pl.ANY)
    vmem = pl.BlockSpec(memory_space=pltpu.VMEM)
    return pl.pallas_call(
        kernel,
        out_shape=(
            jax.ShapeDtypeStruct((4, NT), F32),
            jax.ShapeDtypeStruct((NT, 512), F32),
        ),
        in_specs=[hbm, hbm, hbm, hbm],
        out_specs=(vmem, vmem),
        scratch_shapes=scratch,
        compiler_params=pltpu.CompilerParams(
            collective_id=0, has_side_effects=True, vmem_limit_bytes=55040 * 1024
        ),
    )(output_gradient, adapter_activations.T, proj, labels.reshape(1, 4))


def solution(mesh):
    placed = (P("dp", "param"), P("dp", None), P(("param", "dp"), None, None), P("dp"))
    return jax.shard_map(
        body,
        mesh=mesh,
        in_specs=placed,
        out_specs=(P("dp", None), P(None, "param")),
        check_vma=False,
    )
```
